32 devices in a mesh: rep: 4 (over y, core), fsdp: 8 (over z, x).
Axes of the slice: x: 2, y: 2, z: 4, core: 2. Of those that a mesh axis runs over, the one named last changes fastest.
Arguments:
- tokens: bfloat16 [64, 512, 768], P(('rep', 'fsdp')), may hold values from -6 to 6
- encoder_states: bfloat16 [64, 512, 768], P(('rep', 'fsdp')), may hold values from -6 to 6
- cotangent: bfloat16 [64, 512, 768], P(('rep', 'fsdp')), may hold values from -6 to 6
- qkv_weight: bfloat16 [1, 2, 3, 768, 768], P(None, None, None, 'fsdp'), may hold values from -0.109375 to 0.109375
- out_weight: bfloat16 [1, 2, 768, 768], P(None, None, 'fsdp'), may hold values from -0.625 to 0.625
- ffin_weight: bfloat16 [1, 2, 768, 2048], P(None, None, 'fsdp'), may hold values from -0.21875 to 0.21875
- ffout_weight: bfloat16 [1, 2048, 768], P(None, 'fsdp'), may hold values from -0.125 to 0.125
- norm_gains: bfloat16 [1, 3, 768], P(None, None, 'fsdp'), may hold values from 0.3984375 to 1.59375
- bias_table: bfloat16 [32, 12], P('fsdp'), may hold values from -4 to 4
- lengths: int32 [64], P(('rep', 'fsdp')), may hold values from 65 to 512, as said below
- enc_lengths: int32 [64], P(('rep', 'fsdp')), may hold values from 65 to 512, as said below
Outputs:
- output_state: float32 [64, 512, 768], P(('rep', 'fsdp'))
- token_grad: float32 [64, 512, 768], P(('rep', 'fsdp'))
- encoder_grad: float32 [64, 512, 768], P(('rep', 'fsdp'))
- qkv_grad: float32 [1, 2, 3, 768, 768], P(None, None, None, 'fsdp')
- out_grad: float32 [1, 2, 768, 768], P(None, None, 'fsdp')
- ffin_grad: float32 [1, 2, 768, 2048], P(None, None, 'fsdp')
- ffout_grad: float32 [1, 2048, 768], P(None, 'fsdp')
- gain_grad: float32 [1, 3, 768], P(None, None, 'fsdp')
- table_grad: float32 [32, 12], P('fsdp')
The draws below stay inside these ranges and needn't reach their ends.
Inputs may be any that keep to these rules, and one draw needn't show every extreme that they name: `lengths`: some sequence has exactly 512 live tokens. `enc_lengths`: some sequence has exactly 512 live encoder states.
All inputs are finite; a program needn't handle non-finite values.
Results may differ from the reference program's by a relative error of at most 0.024.
The reference program's roundings to bfloat16 on the way count: a program that leaves them out, or rounds other values in their place, can miss the bound.
Values may be sent and summed in bfloat16 or wider, within the bound.
No kernel may reach another device: no remote copies, remote signals or barrier semaphores. Data moves between devices by JAX's collectives and lax.ppermute only.
A program may use at most 256 MiB of HBM per device.

```python
import jax
import jax.numpy as jnp
from jax import lax

D = 768
H = 12
HD = 64
FF = 2048
NB = 32
DECODER_LAYERS = 1
LEN = 512
ELEN = 512
SEQS = 64


def draw_lengths(key, part):
    key = jax.random.fold_in(key, 11)
    draw_key, pick_key = jax.random.split(key)
    sampled = jax.random.randint(draw_key, (SEQS,), LEN // 8 + 1, LEN + 1)
    chosen = jax.random.randint(pick_key, (), 0, SEQS)
    return jnp.where(jnp.arange(SEQS) == chosen, LEN, sampled).astype(jnp.int32)


def draw_enc_lengths(key, part):
    key = jax.random.fold_in(key, 23)
    draw_key, pick_key = jax.random.split(key)
    sampled = jax.random.randint(draw_key, (SEQS,), ELEN // 8 + 1, ELEN + 1)
    chosen = jax.random.randint(pick_key, (), 0, SEQS)
    return jnp.where(jnp.arange(SEQS) == chosen, ELEN, sampled).astype(jnp.int32)


def block_levels(key, shape, cuts, least, top_value):
    factor_of = 1.0
    for dim, shards_of in cuts:
        steps = jax.random.uniform(jax.random.fold_in(jax.random.fold_in(key, 6), dim), (shards_of,), jnp.float32, least / len(cuts), top_value / len(cuts))
        factor_of = factor_of * jnp.repeat(jnp.exp(steps), shape[dim] // shards_of).reshape((-1,) + (1,) * (len(shape) - 1 - dim))
    return factor_of


def scatter_about(stream_key, dims, deviation, reach, cuts=(), kind=jnp.bfloat16):
    result = deviation * jax.random.normal(stream_key, dims, jnp.float32)
    if cuts:
        result = result * block_levels(stream_key, dims, cuts, -0.22, 0.18)
    return jnp.clip(result, -reach, reach).astype(kind)


def setup_inputs(seed: int = 0) -> dict:
    seeds = jax.random.split(jax.random.key(seed), 12)
    tokens = scatter_about(seeds[0], (SEQS, LEN, D), 1.0, 6.0, ((0, 32),))
    encoder_states = scatter_about(seeds[1], (SEQS, ELEN, D), 1.0, 6.0, ((0, 32),))
    cotangent = scatter_about(seeds[2], (SEQS, LEN, D), 1.0, 6.0, ((0, 32),))
    qkv_weight = scatter_about(seeds[3], (DECODER_LAYERS, 2, 3, D, D), (4 * D) ** -0.5, 0.109375, ((3, 8),))
    out_weight = scatter_about(seeds[4], (DECODER_LAYERS, 2, D, D), (D // 8) ** -0.5, 0.625, ((2, 8),))
    ffin_weight = scatter_about(seeds[5], (DECODER_LAYERS, 2, D, FF), D ** -0.5, 0.21875, ((2, 8),))
    ffout_weight = scatter_about(seeds[6], (DECODER_LAYERS, FF, D), FF ** -0.5, 0.125, ((1, 8),))
    norm_gains = jnp.clip(1.0 + 0.12 * jax.random.normal(seeds[7], (DECODER_LAYERS, 3, D), jnp.float32), 0.3984375, 1.59375).astype(jnp.bfloat16)
    bias_table = scatter_about(seeds[8], (NB, H), 1.0, 4.0, ((0, 8),))
    lengths = draw_lengths(jax.random.fold_in(seeds[11], 71), 0)
    enc_lengths = draw_enc_lengths(jax.random.fold_in(seeds[11], 71), 0)
    return dict(tokens=tokens, encoder_states=encoder_states, cotangent=cotangent, qkv_weight=qkv_weight, out_weight=out_weight, ffin_weight=ffin_weight, ffout_weight=ffout_weight, norm_gains=norm_gains, bias_table=bias_table, lengths=lengths, enc_lengths=enc_lengths)


EPS = 1e-06
NEGATIVE = -1e+30
STEPS = (19, 21, 24, 27, 31, 35, 40, 46, 52, 59, 67, 77, 87, 99, 113)

@jax.custom_vjp
def low(v):
    return lax.optimization_barrier(v.astype(jnp.bfloat16)).astype(jnp.float32)

@jax.custom_vjp
def low_back(v):
    return v

def low_keep(v):
    return (low(v), None)

def low_pass(kept, grad):
    return (grad,)

def back_keep(v):
    return (v, None)

def back_low(kept, grad):
    return (low(grad),)
low.defvjp(low_keep, low_pass)
low_back.defvjp(back_keep, back_low)

def highest(left_operand, right_operand):
    return jnp.dot(left_operand, right_operand, precision=lax.Precision.HIGHEST, preferred_element_type=jnp.float32)

def buckets(extent):
    position = jnp.arange(extent, dtype=jnp.int32)
    distance = jnp.maximum(position[:, None] - position[None, :], 0)
    far_bucket = 16 + sum(((distance >= border).astype(jnp.int32) for border in STEPS))
    return jnp.where(distance < 16, distance, far_bucket).astype(jnp.int32)

def rms_scale(values, factor):
    return values * lax.rsqrt(lax.optimization_barrier(jnp.mean(values * values, axis=-1, keepdims=True)) + EPS) * factor

def attend(query_in, key_in, w_query, w_key, w_value, w_output, extra_bias, allowed):
    query_rows = query_in.shape[0]
    key_rows = key_in.shape[0]
    queries = low_back(low(highest(query_in, w_query))).reshape(query_rows, H, HD)
    key_heads = low_back(low(highest(key_in, w_key))).reshape(key_rows, H, HD)
    value_heads = low_back(low(highest(key_in, w_value))).reshape(key_rows, H, HD)
    scores = jnp.einsum('qhd,khd->hqk', queries, key_heads, precision=lax.Precision.HIGHEST) + extra_bias
    scores = low_back(scores)
    scores = jnp.where(allowed[None], scores, NEGATIVE)
    top_score = lax.optimization_barrier(jnp.max(scores, axis=-1, keepdims=True))
    expanded = jnp.exp(scores - top_score)
    chances = low(expanded / lax.optimization_barrier(jnp.sum(expanded, axis=-1, keepdims=True)))
    mixture = jnp.einsum('hqk,khd->qhd', chances, value_heads, precision=lax.Precision.HIGHEST)
    mixture = low_back(low(mixture.reshape(query_rows, H * HD)))
    return low_back(highest(mixture, w_output))

def reference(tokens, encoder_states, cotangent, qkv_weight, out_weight, ffin_weight, ffout_weight, norm_gains, bias_table, lengths, enc_lengths):
    position = jnp.arange(LEN, dtype=jnp.int32)
    enc_position = jnp.arange(ELEN, dtype=jnp.int32)

    def forward(tokens_all, encoder_all, qkv_all, out_all, ffin_all, ffout_all, gains_all, table_all):
        extra_bias = jnp.transpose(table_all[buckets(LEN)], (2, 0, 1))

        def sequence(packed):
            stream, encoder_one, live_length, enc_length = packed
            causal = (position[None, :] <= position[:, None]) & (position[None, :] < live_length)
            visible = jnp.broadcast_to(enc_position[None, :] < enc_length, (LEN, ELEN))
            for layer_index in range(DECODER_LAYERS):
                normed = low(rms_scale(stream, gains_all[layer_index, 0]))
                stream = stream + attend(normed, normed, qkv_all[layer_index, 0, 0], qkv_all[layer_index, 0, 1], qkv_all[layer_index, 0, 2], out_all[layer_index, 0], extra_bias, causal)
                normed = low(rms_scale(stream, gains_all[layer_index, 1]))
                stream = stream + attend(normed, encoder_one, qkv_all[layer_index, 1, 0], qkv_all[layer_index, 1, 1], qkv_all[layer_index, 1, 2], out_all[layer_index, 1], jnp.float32(0.0), visible)
                normed = low(rms_scale(stream, gains_all[layer_index, 2]))
                gate = low_back(highest(normed, ffin_all[layer_index, 0]))
                upward = low_back(highest(normed, ffin_all[layer_index, 1]))
                product = low(jax.nn.gelu(gate, approximate=True) * upward)
                stream = stream + low_back(highest(product, ffout_all[layer_index]))
            return stream * (position < live_length).astype(jnp.float32)[:, None]
        return lax.map(jax.checkpoint(sequence), (tokens_all, encoder_all, lengths, enc_lengths))
    primal = (tokens.astype(jnp.float32), encoder_states.astype(jnp.float32), qkv_weight.astype(jnp.float32), out_weight.astype(jnp.float32), ffin_weight.astype(jnp.float32), ffout_weight.astype(jnp.float32), norm_gains.astype(jnp.float32), bias_table.astype(jnp.float32))
    output, pullback = jax.vjp(forward, *primal)
    gradients = pullback(cotangent.astype(jnp.float32))
    return (output, gradients[0], gradients[1], gradients[2], gradients[3], gradients[4], gradients[5], gradients[6], gradients[7])
```

```python
import functools

import jax
import jax.numpy as jnp
from jax import lax
from jax.experimental import pallas as pl
from jax.experimental.pallas import tpu as pltpu
from jax.sharding import PartitionSpec as P

EPS = 1e-06
STEPS = (19, 21, 24, 27, 31, 35, 40, 46, 52, 59, 67, 77, 87, 99, 113)


Z = 4


class Place:
    def __init__(self, rep, fsdp):
        self.rep, self.fsdp = rep, fsdp
        self.nx = fsdp // Z
        r = lax.axis_index("rep")
        f = lax.axis_index("fsdp")
        self.c, self.y = r % 2, (r // 2) % 2
        self.z, self.x = f // self.nx, f % self.nx
        self.q = 2 * self.y + self.c

    def core(self, v):
        return lax.ppermute(v, "rep", [(i, i ^ 1) for i in range(self.rep)])

    def across(self, v, bit):
        return lax.ppermute(v, "rep", [(i, i ^ bit) for i in range(self.rep)])

    def along_x(self, v, d):
        nx = self.nx
        return lax.ppermute(
            v, "fsdp", [(i, i // nx * nx + (i % nx + d) % nx) for i in range(self.fsdp)]
        )

    def along_z(self, v, d):
        return lax.ppermute(
            v, "fsdp", [(i, (i + d * self.nx) % self.fsdp) for i in range(self.fsdp)]
        )


def low(v):
    return v.astype(jnp.bfloat16)


def wide(v):
    return v.astype(jnp.float32)


def pick(v, i, axis=0):
    return lax.dynamic_index_in_dim(v, i, axis, keepdims=False)


def assemble_kernel(where_ref, *refs, parts, nx, kind):
    out = refs[-1]
    c, y, z, x = (where_ref[i] for i in range(4))
    for ref, (dc, dy, dx) in zip(refs, parts):
        core = c ^ dc
        row = y ^ dy
        col = lax.rem(x - dx + nx, nx)
        width = ref.shape[-1]
        for k in range(Z):
            f = lax.rem(z - k + Z, Z) * nx + col
            if kind == "matrix":
                out[2 * row + core, f] = ref[k]
            elif kind == "columns":
                out[row, f, :, pl.ds(pl.multiple_of(core * width, width), width)] = ref[k]
            else:
                out[f, core, :, pl.ds(pl.multiple_of(row * width, width), width)] = ref[k]


def gather_stage(place, piece, kind, y_last):
    rows, cols = piece.shape
    nx, fsdp = place.nx, place.fsdp
    stack = jnp.stack([piece] + [place.along_z(piece, d) for d in range(1, Z)])
    held = {(0, 0): stack}
    if y_last:
        for d in range(1, nx):
            held[0, d] = place.along_x(stack, d)
        for d in range(nx):
            held[1, d] = place.across(held[0, d], 2)
    else:
        held[1, 0] = place.across(stack, 2)
        for d in range(1, nx):
            for e in range(2):
                held[e, d] = place.along_x(held[e, 0], d)
    parts, arrays = [], []
    for (e, d), value in held.items():
        parts += [(0, e, d), (1, e, d)]
        arrays += [value, place.across(value, 1)]
    shape = {
        "matrix": (4, fsdp, rows, cols),
        "columns": (2, fsdp, rows, 2 * cols),
        "corners": (fsdp, 2, rows, 2 * cols),
    }[kind]
    where = jnp.stack([place.c, place.y, place.z, place.x]).astype(jnp.int32)
    return pl.pallas_call(
        functools.partial(assemble_kernel, parts=tuple(parts), nx=nx, kind=kind),
        out_shape=jax.ShapeDtypeStruct(shape, piece.dtype),
        in_specs=[pl.BlockSpec(memory_space=pltpu.SMEM)]
        + [pl.BlockSpec(memory_space=pltpu.VMEM)] * len(arrays),
        out_specs=pl.BlockSpec(memory_space=pltpu.VMEM),
        name="assemble_" + kind,
        compiler_params=pltpu.CompilerParams(vmem_limit_bytes=40 * 1024 * 1024),
        cost_estimate=pl.CostEstimate(
            flops=0, bytes_accessed=2 * 4 * fsdp * rows * cols * 2, transcendentals=0
        ),
    )(where, *arrays)


def gather_small(place, piece):
    nx = place.nx
    near = [piece] + [place.along_x(piece, nx - d) for d in range(1, nx)]
    near = jnp.roll(jnp.stack(near), place.x, axis=0)
    far = [near] + [place.along_z(near, Z - d) for d in range(1, Z)]
    return jnp.roll(jnp.stack(far), place.z, axis=0).reshape((place.fsdp,) + piece.shape)


def over_z(place, acc):
    total = pick(acc, place.z)
    for d in range(1, Z):
        total = total + wide(place.along_z(low(pick(acc, (place.z + d) % Z)), d))
    return total


def reduce_stage(place, sent, kept, y_first):
    nx = place.nx
    shape = (Z, nx) + sent[0].shape[1:]
    acc = [k + wide(place.across(s, 1)) for s, k in zip(sent, kept)]
    acc = [a.reshape(shape) for a in acc]
    own_y = place.y == 0
    if y_first:
        part = jnp.where(own_y, acc[0], acc[1])
        part = part + wide(place.across(low(jnp.where(own_y, acc[1], acc[0])), 2))
        total = pick(part, place.x, 1)
        for d in range(1, nx):
            total = total + wide(place.along_x(low(pick(part, (place.x + d) % nx, 1)), d))
    else:
        part = jnp.stack([pick(a, place.x, 1) for a in acc])
        for d in range(1, nx):
            away = (place.x + d) % nx
            part = part + wide(place.along_x(jnp.stack([low(pick(a, away, 1)) for a in acc]), d))
        total = pick(part, place.y) + wide(place.across(low(pick(part, 1 - place.y)), 2))
    total = over_z(place, total)
    bit = 4
    while bit < place.rep:
        total = total + place.across(total, bit)
        bit *= 2
    other = place.across(total, 2)
    pair = jnp.stack([jnp.where(own_y, total, other), jnp.where(own_y, other, total)])
    mate = place.across(pair, 1)
    by_core = (jnp.where(place.c == 0, pair, mate), jnp.where(place.c == 0, mate, pair))
    return [[by_core[c][y] for c in range(2)] for y in range(2)]


def reduce_small(place, partial):
    total = partial
    bit = 1
    while bit < place.rep:
        total = total + place.across(total, bit)
        bit *= 2
    total = total.reshape(Z, place.nx, -1)
    near = pick(total, place.x, 1)
    for d in range(1, place.nx):
        near = near + place.along_x(pick(total, (place.x + d) % place.nx, 1), d)
    mine = pick(near, place.z)
    for d in range(1, Z):
        mine = mine + place.along_z(pick(near, (place.z + d) % Z), d)
    return mine


NEGATIVE = -1e30
TILE = 256
PAIR = 128


def dot(a, b, dims):
    return lax.dot_general(a, b, (dims, ((), ())), preferred_element_type=jnp.float32)


NT = ((1,), (1,))
NN = ((1,), (0,))


def turned(v):
    return v.astype(jnp.float32).T


def half_mask(j):
    return lax.broadcasted_iota(jnp.int32, (1, PAIR), 1) // (PAIR // 2) == j


def masked_scores(k, qm, toe, length, t, causal):
    scores = dot(k, qm, NT)
    rows = scores.shape[0]
    key = lax.broadcasted_iota(jnp.int32, (rows, TILE), 0)
    if causal:
        bias = toe[:, :TILE]
        if t:
            bias = jnp.concatenate([toe[:, TILE:], bias], axis=0)
        scores = scores + bias
        query = lax.broadcasted_iota(jnp.int32, (rows, TILE), 1) + t * TILE
        allowed = key <= jnp.minimum(query, length - 1)
    else:
        allowed = key < length
    return jnp.where(allowed, scores, NEGATIVE)


def spread(row_ref, toe_ref):
    for j in range(2):
        row = jnp.broadcast_to(row_ref[0, j : j + 1, :], (TILE, 2 * TILE))
        toe_ref[j] = pltpu.roll(row, 0, 1, stride=1, stride_axis=0)


def forward_kernel(causal, len_ref, *refs):
    if causal:
        q_ref, k_ref, v_ref, row_ref, o_ref, lse_ref, toe_ref = refs
    else:
        q_ref, k_ref, v_ref, o_ref, lse_ref = refs
        toe_ref = None
    s = pl.program_id(1)
    length = len_ref[s]
    if causal:

        @pl.when(s == 0)
        def _():
            spread(row_ref, toe_ref)

    q, k, v = q_ref[0], k_ref[0], v_ref[0]
    v_turned = turned(v).astype(jnp.bfloat16)
    for t in range(q.shape[0] // TILE):
        seen = (t + 1) * TILE if causal else k.shape[0]
        here = slice(t * TILE, (t + 1) * TILE)
        outs = []
        for j in range(2):
            qm = jnp.where(half_mask(j), q[here], 0)
            scores = masked_scores(k[:seen], qm, toe_ref[j] if causal else None, length, t, causal)
            top = jnp.max(scores, axis=0, keepdims=True)
            grown = jnp.exp(scores - top)
            total = jnp.sum(grown, axis=0, keepdims=True)
            chances = (grown * (1.0 / total)).astype(jnp.bfloat16)
            lse_ref[0, 0, j : j + 1, here] = top + jnp.log(total)
            outs.append(dot(v_turned[j * 64 : (j + 1) * 64, :seen], chances, NN))
        o_ref[0, here, :] = turned(jnp.concatenate(outs, axis=0)).astype(jnp.bfloat16)


def diagonal_sums(v):
    width = v.shape[1]
    groups = v[:8]
    for a in range(8, v.shape[0], 8):
        groups = groups + pltpu.roll(v[a : a + 8], width - a, 1)
    total = groups[:1]
    for b in range(1, 8):
        total = total + pltpu.roll(groups[b : b + 1], width - b, 1)
    return total


def backward_kernel(causal, len_ref, *refs):
    if causal:
        q_ref, k_ref, v_ref, do_ref, lse_ref, row_ref = refs[:6]
        dq_ref, dk_ref, dv_ref, diag_ref, toe_ref, sum_ref = refs[6:]
    else:
        q_ref, k_ref, v_ref, do_ref, lse_ref = refs[:5]
        dq_ref, dk_ref, dv_ref = refs[5:]
        toe_ref = None
    s = pl.program_id(1)
    length = len_ref[s]
    if causal:

        @pl.when(s == 0)
        def _():
            spread(row_ref, toe_ref)
            sum_ref[...] = jnp.zeros_like(sum_ref)

    q, k, v, do = q_ref[0], k_ref[0], v_ref[0], do_ref[0]
    k_turned = turned(k).astype(jnp.bfloat16)
    tiles = q.shape[0] // TILE
    dk = [None] * tiles
    dv = [None] * tiles

    def add(held, value):
        return value if held is None else held + value

    for t in range(tiles):
        seen = (t + 1) * TILE if causal else k.shape[0]
        here = slice(t * TILE, (t + 1) * TILE)
        outs = []
        for j in range(2):
            qm = jnp.where(half_mask(j), q[here], 0)
            dom = jnp.where(half_mask(j), do[here], 0)
            scores = masked_scores(k[:seen], qm, toe_ref[j] if causal else None, length, t, causal)
            chances = jnp.exp(scores - lse_ref[0, 0, j : j + 1, here])
            d_chances = dot(v[:seen], dom, NT)
            delta = jnp.sum(chances * d_chances, axis=0, keepdims=True)
            d_scores = (chances * (d_chances - delta)).astype(jnp.bfloat16)
            outs.append(dot(k_turned[j * 64 : (j + 1) * 64, :seen], d_scores, NN))
            dv_part = dot(chances.astype(jnp.bfloat16), dom, NN)
            dk_part = dot(d_scores, qm, NN)
            for b in range(seen // TILE):
                rows = slice(b * TILE, (b + 1) * TILE)
                dv[b] = add(dv[b], dv_part[rows])
                dk[b] = add(dk[b], dk_part[rows])
            if causal:
                if t:
                    sum_ref[j, :, TILE:] += d_scores[: t * TILE].astype(jnp.float32)
                sum_ref[j, :, :TILE] += d_scores[t * TILE :].astype(jnp.float32)
        dq_ref[0, here, :] = turned(jnp.concatenate(outs, axis=0)).astype(jnp.bfloat16)
    for b in range(tiles):
        rows = slice(b * TILE, (b + 1) * TILE)
        dk_ref[0, rows, :] = dk[b].astype(jnp.bfloat16)
        dv_ref[0, rows, :] = dv[b].astype(jnp.bfloat16)
    if causal:

        @pl.when(s == pl.num_programs(1) - 1)
        def _():
            for j in range(2):
                diag_ref[0, j : j + 1, :] = diagonal_sums(sum_ref[j])


def attend(kind, q, k, v, lengths, row=None, do=None, lse=None):
    count, slots, width = q.shape
    pairs = width // PAIR
    assert slots == 2 * TILE and k.shape[1] == 2 * TILE
    block = pl.BlockSpec((1, slots, PAIR), lambda p, s: (s, 0, p))
    lse_block = pl.BlockSpec((1, 1, 2, slots), lambda p, s: (s, p, 0, 0))
    row_block = pl.BlockSpec((1, 2, slots), lambda p, s: (p, 0, 0))
    state = jax.ShapeDtypeStruct(q.shape, jnp.bfloat16)
    causal = row is not None
    ins, specs = [lengths, q, k, v], [pl.BlockSpec(memory_space=pltpu.SMEM), block, block, block]
    if kind == "forward":
        body = forward_kernel
        outs = [state, jax.ShapeDtypeStruct((count, pairs, 2, slots), jnp.float32)]
        out_specs = [block, lse_block]
        dots = 2
    else:
        body = backward_kernel
        ins += [do, lse]
        specs += [block, lse_block]
        outs = [state] * 3
        out_specs = [block] * 3
        dots = 5
    scratch = []
    if causal:
        ins.append(row)
        specs.append(row_block)
        scratch.append(pltpu.VMEM((2, TILE, 2 * TILE), jnp.float32))
        if kind == "backward":
            outs.append(jax.ShapeDtypeStruct(row.shape, jnp.float32))
            out_specs.append(row_block)
            scratch.append(pltpu.VMEM((2, TILE, 2 * TILE), jnp.float32))
    work = count * slots * slots * width
    return pl.pallas_call(
        functools.partial(body, causal),
        grid=(pairs, count),
        in_specs=specs,
        out_specs=out_specs,
        out_shape=outs,
        scratch_shapes=scratch,
        name=("self_" if causal else "cross_") + kind,
        compiler_params=pltpu.CompilerParams(vmem_limit_bytes=40 * 1024 * 1024),
        cost_estimate=pl.CostEstimate(
            flops=4 * dots * work, bytes_accessed=2 * q.size * 10, transcendentals=work // 64
        ),
    )(*ins)


def rms_scale(values, factor):
    return values * lax.rsqrt(jnp.mean(values * values, axis=-1, keepdims=True) + EPS) * factor


def rms_back(values, factor, grad_out):
    return jax.vjp(rms_scale, values, factor)[1](grad_out)


def geglu(gate_in, upward_in):
    return jax.nn.gelu(gate_in, approximate=True) * upward_in


def project(a, w):
    return jnp.einsum("vgq,qy->vgy", a, w, preferred_element_type=jnp.float32)


def project_back(a, w):
    return jnp.einsum("gjr,fr->gjf", a, w, preferred_element_type=jnp.float32)


def weight_grad(a, b):
    return jnp.einsum("nou,noi->ui", a, b, preferred_element_type=jnp.float32)


def bucket_hot(extent, buckets):
    distance = jnp.arange(extent, dtype=jnp.int32)
    far = 16 + sum(((distance >= border).astype(jnp.int32) for border in STEPS))
    bucket = jnp.where(distance < 16, distance, far)
    return (bucket[:, None] == jnp.arange(buckets, dtype=jnp.int32)).astype(jnp.float32)


def per_device(
    rep,
    fsdp,
    tokens,
    encoder_states,
    cotangent,
    qkv_weight,
    out_weight,
    ffin_weight,
    ffout_weight,
    norm_gains,
    bias_table,
    lengths,
    enc_lengths,
):
    place = Place(rep, fsdp)
    seq_len, width = tokens.shape[1:]
    table_rows, heads = bias_table.shape
    shard = qkv_weight.shape[3]
    first = place.c == 0

    def choose(a, b):
        return jnp.where(first, a, b)

    def attention_piece(i):
        return pick(jnp.concatenate([qkv_weight[0, i], out_weight[0, i : i + 1]]), place.q)

    self_w = gather_stage(place, attention_piece(0), "matrix", True)
    small_count = 3 * shard + table_rows * heads
    small = jnp.concatenate([norm_gains.reshape(-1), bias_table.reshape(-1)])
    small = gather_small(place, jnp.pad(small, (0, -small_count % 128)))
    gains = small[:, : 3 * shard].reshape(fsdp, 3, shard)
    gains = wide(jnp.transpose(gains, (1, 0, 2)).reshape(3, width))
    table = wide(small[:, 3 * shard : small_count].reshape(fsdp * table_rows, heads))
    cross_w = gather_stage(place, attention_piece(1), "matrix", False)
    half = ffin_weight.shape[3] // 2
    piece = lax.dynamic_slice(
        ffin_weight[0], (place.y, 0, place.c * half), (1, shard, half)
    )[0]
    ffin = gather_stage(place, piece, "columns", True)
    corner = (ffout_weight.shape[1] // 2, width // 2)
    piece = lax.dynamic_slice(
        ffout_weight[0], (place.c * corner[0], place.y * corner[1]), corner
    )
    ffout = gather_stage(place, piece, "corners", False)
    self_w = self_w.reshape(4, width, width)
    cross_w = cross_w.reshape(4, width, width)
    ffin = ffin.reshape(2, width, 2 * half)
    ffout = ffout.reshape(2 * half, width)

    live = wide(jnp.arange(seq_len, dtype=jnp.int32)[None, :] < lengths[:, None])[:, :, None]
    hot = bucket_hot(seq_len, fsdp * table_rows)
    row = jnp.einsum("nb,bh->hn", hot, table, precision=lax.Precision.HIGHEST)
    row = row.reshape(heads // 2, 2, seq_len)
    stream = wide(tokens)
    normed_self = low(rms_scale(stream, gains[0]))
    q1, k1, v1 = (low(project(normed_self, self_w[i])) for i in range(3))
    o1, lse1 = attend("forward", q1, k1, v1, lengths, row)
    middle = stream + project(o1, self_w[3])
    normed_cross = low(rms_scale(middle, gains[1]))
    q2 = low(project(normed_cross, cross_w[0]))
    k2, v2 = (low(project(encoder_states, cross_w[i])) for i in (1, 2))
    o2, lse2 = attend("forward", q2, k2, v2, enc_lengths)
    later = middle + project(o2, cross_w[3])
    normed_feed = low(rms_scale(later, gains[2]))
    gate = project(normed_feed, ffin[0])
    upward = project(normed_feed, ffin[1])
    product = low(geglu(gate, upward))
    output_state = (later + project(product, ffout)) * live

    grad = wide(cotangent) * live
    grad_low = low(grad)
    grad_product = project_back(grad_low, ffout)
    grad_gate, grad_upward = jax.vjp(geglu, gate, upward)[1](grad_product)
    grad_gate, grad_upward = low(grad_gate), low(grad_upward)
    cells = product.reshape(product.shape[:2] + (fsdp, 2, corner[0]))
    near, far = (cells[:, :, :, c].reshape(product.shape[:2] + (half,)) for c in range(2))

    def ffout_parts(left):
        return [
            weight_grad(left, grad_low[:, :, y * corner[1] : (y + 1) * corner[1]]).reshape(
                (fsdp,) + corner
            )
            for y in range(2)
        ]

    ffout_done = reduce_stage(
        place,
        [low(p) for p in ffout_parts(choose(far, near))],
        ffout_parts(choose(near, far)),
        True,
    )

    def ffin_parts(c_first):
        return [
            weight_grad(
                normed_feed, jnp.where(c_first, g[:, :, :half], g[:, :, half:])
            ).reshape(fsdp, shard, half)
            for g in (grad_gate, grad_upward)
        ]

    ffin_done = reduce_stage(
        place,
        [low(p) for p in ffin_parts(place.c == 1)],
        ffin_parts(first),
        False,
    )
    grad_normed = project_back(grad_gate, ffin[0]) + project_back(grad_upward, ffin[1])
    grad_norm, gain_feed = rms_back(later, gains[2], grad_normed)
    grad_later = grad + grad_norm

    def attention_parts(c_first, y0, y1):
        return [
            weight_grad(
                *(a if a is b else jnp.where(c_first, a, b) for a, b in zip(*both))
            ).reshape(fsdp, shard, width)
            for both in (y0, y1)
        ]

    def attention_reduce(y0, y1, y_first):
        return reduce_stage(
            place,
            [low(p) for p in attention_parts(place.c == 1, y0, y1)],
            attention_parts(first, y0, y1),
            y_first,
        )

    da = low(grad_later)
    do = low(project_back(da, cross_w[3]))
    dq, dk, dv = attend("backward", q2, k2, v2, enc_lengths, None, do, lse2)
    cross_done = attention_reduce(
        ((normed_cross, dq), (encoder_states, dk)), ((encoder_states, dv), (o2, da)), True
    )
    encoder_grad = project_back(dk, cross_w[1]) + project_back(dv, cross_w[2])
    grad_norm, gain_cross = rms_back(middle, gains[1], project_back(dq, cross_w[0]))
    grad_middle = grad_later + grad_norm

    da = low(grad_middle)
    do = low(project_back(da, self_w[3]))
    dq, dk, dv, diagonals = attend("backward", q1, k1, v1, lengths, row, do, lse1)
    self_done = attention_reduce(
        ((normed_self, dq), (normed_self, dk)), ((normed_self, dv), (o1, da)), False
    )
    into = project_back(dq, self_w[0]) + project_back(dk, self_w[1]) + project_back(dv, self_w[2])
    grad_norm, gain_self = rms_back(stream, gains[0], into)
    token_grad = grad_middle + grad_norm
    grad_table = jnp.einsum(
        "nb,hn->bh", hot, diagonals.reshape(heads, seq_len), precision=lax.Precision.HIGHEST
    )

    small = jnp.stack([gain_self, gain_cross, gain_feed]).reshape(3, fsdp, shard)
    small = jnp.concatenate(
        [
            jnp.transpose(small, (1, 0, 2)).reshape(fsdp, 3 * shard),
            grad_table.reshape(fsdp, table_rows * heads),
        ],
        axis=1,
    )
    small = reduce_small(place, jnp.pad(small, ((0, 0), (0, -small_count % 128))))

    done = (self_done, cross_done)
    qkv_grad = jnp.stack([jnp.stack([d[0][0], d[0][1], d[1][0]]) for d in done])[None]
    out_grad = jnp.stack([d[1][1] for d in done])[None]
    ffin_grad = jnp.stack([jnp.concatenate(g, axis=1) for g in ffin_done])[None]
    ffout_grad = jnp.concatenate(
        [jnp.concatenate([ffout_done[0][c], ffout_done[1][c]], axis=1) for c in range(2)]
    )[None]
    return (
        output_state,
        token_grad,
        encoder_grad,
        qkv_grad,
        out_grad,
        ffin_grad,
        ffout_grad,
        small[: 3 * shard].reshape(1, 3, shard),
        small[3 * shard : small_count].reshape(table_rows, heads),
    )


def solution(mesh):
    in_specs = (
        P(("rep", "fsdp"), None, None),
        P(("rep", "fsdp"), None, None),
        P(("rep", "fsdp"), None, None),
        P(None, None, None, "fsdp", None),
        P(None, None, "fsdp", None),
        P(None, None, "fsdp", None),
        P(None, "fsdp", None),
        P(None, None, "fsdp"),
        P("fsdp", None),
        P(("rep", "fsdp")),
        P(("rep", "fsdp")),
    )
    out_specs = (
        P(("rep", "fsdp"), None, None),
        P(("rep", "fsdp"), None, None),
        P(("rep", "fsdp"), None, None),
        P(None, None, None, "fsdp", None),
        P(None, None, "fsdp", None),
        P(None, None, "fsdp", None),
        P(None, "fsdp", None),
        P(None, None, "fsdp"),
        P("fsdp", None),
    )
    return jax.shard_map(
        functools.partial(per_device, mesh.shape["rep"], mesh.shape["fsdp"]),
        mesh=mesh, in_specs=in_specs, out_specs=out_specs, check_vma=False
    )
```

```python
import functools

import jax
import jax.numpy as jnp
from jax import lax
from jax.experimental import pallas as pl
from jax.experimental.pallas import tpu as pltpu
from jax.sharding import PartitionSpec as P

EPS = 1e-06
STEPS = (19, 21, 24, 27, 31, 35, 40, 46, 52, 59, 67, 77, 87, 99, 113)


Z = 4


class Place:
    def __init__(self, rep, fsdp):
        self.rep, self.fsdp = rep, fsdp
        self.nx = fsdp // Z
        r = lax.axis_index("rep")
        f = lax.axis_index("fsdp")
        self.c, self.y = r % 2, (r // 2) % 2
        self.z, self.x = f // self.nx, f % self.nx
        self.q = 2 * self.y + self.c

    def core(self, v):
        return lax.ppermute(v, "rep", [(i, i ^ 1) for i in range(self.rep)])

    def across(self, v, bit):
        return lax.ppermute(v, "rep", [(i, i ^ bit) for i in range(self.rep)])

    def along_x(self, v, d):
        nx = self.nx
        return lax.ppermute(
            v, "fsdp", [(i, i // nx * nx + (i % nx + d) % nx) for i in range(self.fsdp)]
        )

    def along_z(self, v, d):
        return lax.ppermute(
            v, "fsdp", [(i, (i + d * self.nx) % self.fsdp) for i in range(self.fsdp)]
        )


def low(v):
    return v.astype(jnp.bfloat16)


def wide(v):
    return v.astype(jnp.float32)


def pick(v, i, axis=0):
    return lax.dynamic_index_in_dim(v, i, axis, keepdims=False)


FREE = pl.CostEstimate(flops=0, bytes_accessed=0, transcendentals=0)


def lasting(microseconds):
    return pl.CostEstimate(
        flops=int(microseconds * 1e9), bytes_accessed=0, transcendentals=0
    )


VMEM = pl.BlockSpec(memory_space=pltpu.VMEM)
SMEM = pl.BlockSpec(memory_space=pltpu.SMEM)


def shape_of(shape, dtype=jnp.bfloat16):
    return jax.ShapeDtypeStruct(shape, dtype)


def call(body, ins, outs, name, waits=(), specs=None, vmem=32, cost=FREE, **kw):
    waits = list(waits)
    count, late = len(ins), len(ins) + len(waits)

    def kernel(*refs):
        body(*refs[:count], *refs[late:])

    return pl.pallas_call(
        kernel,
        in_specs=list(specs or [VMEM] * count) + [pl.BlockSpec(memory_space=pl.ANY)] * len(waits),
        out_shape=outs,
        name=name,
        compiler_params=pltpu.CompilerParams(vmem_limit_bytes=vmem * 1024 * 1024),
        cost_estimate=cost,
        **kw,
    )(*ins, *waits)


def stack_kernel(*refs):
    for k, ref in enumerate(refs[:-1]):
        refs[-1][k] = ref[...]


def copy_kernel(ref, out):
    out[...] = ref[...]


def stacked(values, waits=()):
    shape = shape_of((len(values),) + values[0].shape, values[0].dtype)
    return call(stack_kernel, values, shape, "stack", waits)


def held_back(value, waits):
    return call(copy_kernel, [value], shape_of(value.shape, value.dtype), "hold", waits)


LANES = 128
SMALL_ROWS = 16


def assemble_kernel(where_ref, *refs, parts, nx, sizes, small):
    outs = refs[len(parts) :]
    c, y, z, x = (where_ref[i] for i in range(4))
    for ref, (dc, dy, dx) in zip(refs, parts):
        core = c ^ dc
        row = y ^ dy
        col = lax.rem(x - dx + nx, nx)
        for k in range(Z):
            f = lax.rem(z - k + Z, Z) * nx + col
            at = 0
            for out, (m, h, w) in zip(outs, sizes):
                for t in range(w // LANES):
                    lane = pl.ds(pl.multiple_of(core * w + t * LANES, LANES), LANES)
                    for i in range(m):
                        out[i, f, row, :, lane] = ref[k, at : at + h, :]
                        at += h
            if small and (dc, dy) == (0, 0):
                outs[-1][f] = ref[k, at : at + SMALL_ROWS, :]


class Gather:
    def __init__(self, place, shards, y_last, small=None):
        self.place, self.y_last, self.small = place, y_last, small
        self.sizes, rows = [], []
        for shard in shards:
            m, h, w = shard.shape[0], shard.shape[1] // 2, shard.shape[2] // 2
            self.sizes.append((m, h, w))
            cut = lax.dynamic_slice(shard, (0, place.y * h, place.c * w), (m, h, w))
            cut = jnp.transpose(cut.reshape(m, h, w // LANES, LANES), (2, 0, 1, 3))
            rows.append(cut.reshape(-1, LANES))
        if small is not None:
            rows.append(small)
        self.piece = rows[0] if len(rows) == 1 else jnp.concatenate(rows)

    def first(self):
        self.pieces = [self.piece] + [self.place.along_z(self.piece, d) for d in range(1, Z)]

    def second(self, *waits):
        self.stack = stacked(self.pieces, waits)

    def send(self):
        place, stack = self.place, self.stack
        self.held = {(0, 0): stack}
        for d in range(1, place.nx):
            self.held[0, d] = place.along_x(stack, d)
        self.held[1, 0] = place.across(stack, 2)

    def turn(self, *waits):
        self.onward = []
        for d in range(1, self.place.nx) if self.y_last else (0,):
            key = (0, d) if self.y_last else (1, 0)
            if waits:
                self.held[key] = held_back(self.held[key], waits)
            self.onward.append(self.held[key])

    def third(self):
        place, nx = self.place, self.place.nx
        for d in range(1, nx):
            if self.y_last:
                self.held[1, d] = place.across(self.held[0, d], 2)
            else:
                self.held[1, d] = place.along_x(self.held[1, 0], d)

    def settle(self, *waits):
        for d in range(1, self.place.nx):
            self.held[1, d] = held_back(self.held[1, d], waits)

    def whole(self, *waits):
        place = self.place
        parts, arrays = [], []
        for key, value in self.held.items():
            parts += [(0,) + key, (1,) + key]
            arrays += [value, place.across(value, 1)]
        shapes = [shape_of((m, place.fsdp, 2, h, 2 * w)) for m, h, w in self.sizes]
        if self.small is not None:
            shapes.append(shape_of((place.fsdp, SMALL_ROWS, LANES)))
        where = jnp.stack([place.c, place.y, place.z, place.x]).astype(jnp.int32)
        body = functools.partial(
            assemble_kernel,
            parts=tuple(parts),
            nx=place.nx,
            sizes=tuple(self.sizes),
            small=self.small is not None,
        )
        specs = [SMEM] + [VMEM] * len(arrays)
        full = call(body, [where] + arrays, shapes, "assemble", waits, specs, vmem=36)
        whole = [
            v.reshape(m, place.fsdp * 2 * h, 2 * w) for v, (m, h, w) in zip(full, self.sizes)
        ]
        return whole + list(full[len(whole) :])


def step_kernel(where_ref, kept_ref, *refs, axis, count, lead):
    got, keep_ref, send_refs = refs[: -count], refs[-count], refs[len(refs) - count + 1 :]
    own = where_ref[0]
    rest = [()]
    for size in lead[:axis] + lead[axis + 1 :]:
        rest = [r + (i,) for r in rest for i in range(size)]

    def value(at):
        total = kept_ref[at]
        for ref in got:
            total = total + ref[at].astype(jnp.float32)
        return total

    for r in rest:
        keep_ref[r] = value(r[:axis] + (own,) + r[axis:])
        for d, ref in enumerate(send_refs, 1):
            there = lax.rem(own + d, count)
            ref[r] = value(r[:axis] + (there,) + r[axis:]).astype(jnp.bfloat16)


def total_kernel(kept_ref, *refs):
    total = kept_ref[...]
    for ref in refs[:-1]:
        total = total + ref[...].astype(jnp.float32)
    refs[-1][...] = total


class Reduce:
    def __init__(self, place, sent, kept):
        self.place = place
        lead = (Z, place.nx, 2)
        self.sent = [sent]
        self.kept = kept.reshape(lead + kept.shape[2:])
        self.axes = ["z", "x", "y"]
        self.name = "core"

    def send(self):
        place = self.place
        if self.name == "core":
            self.got = [place.across(self.sent[0], 1).reshape(self.kept.shape)]
        elif self.name == "y":
            self.got = [place.across(self.sent[0], 2)]
        else:
            move = place.along_x if self.name == "x" else place.along_z
            self.got = [move(v, d) for d, v in enumerate(self.sent, 1)]

    def step(self, name, *waits):
        place = self.place
        axis = self.axes.index(name)
        lead, tail = self.kept.shape[:-2], self.kept.shape[-2:]
        count = lead[axis]
        left = lead[:axis] + lead[axis + 1 :] + tail
        own = {"z": place.z, "x": place.x, "y": place.y}[name].reshape(1).astype(jnp.int32)
        outs = [shape_of(left, jnp.float32)] + [shape_of(left)] * (count - 1)
        body = functools.partial(step_kernel, axis=axis, count=count, lead=lead)
        ins = [own, self.kept] + self.got
        specs = [SMEM] + [VMEM] * (len(ins) - 1)
        self.kept, *self.sent = call(body, ins, outs, "step_" + name, waits, specs)
        self.axes.remove(name)
        self.name = name

    def finish(self, *waits):
        place = self.place
        shape = shape_of(self.kept.shape, jnp.float32)
        total = call(total_kernel, [self.kept] + self.got, shape, "total", waits)
        bit = 4
        while bit < place.rep:
            total = total + place.across(total, bit)
            bit *= 2
        self.total, self.other = total, place.across(total, 2)

    def done(self):
        place = self.place
        own = place.y == 0
        rows = jnp.concatenate(
            [jnp.where(own, self.total, self.other), jnp.where(own, self.other, self.total)]
        )
        mate = place.across(rows, 1)
        return jnp.where(place.c == 0, rows, mate), jnp.where(place.c == 0, mate, rows)


def reduce_small(place, partial):
    total = partial
    bit = 1
    while bit < place.rep:
        total = total + place.across(total, bit)
        bit *= 2
    total = total.reshape(Z, place.nx, -1)
    near = pick(total, place.x, 1)
    for d in range(1, place.nx):
        near = near + place.along_x(pick(total, (place.x + d) % place.nx, 1), d)
    mine = pick(near, place.z)
    for d in range(1, Z):
        mine = mine + place.along_z(pick(near, (place.z + d) % Z), d)
    return mine


NEGATIVE = -1e30
TILE = 256
PAIR = 128


def dot(a, b, dims):
    return lax.dot_general(a, b, (dims, ((), ())), preferred_element_type=jnp.float32)


NT = ((1,), (1,))
NN = ((1,), (0,))
TN = ((0,), (0,))


def turned(v):
    return v.astype(jnp.float32).T


def half_mask(j):
    return lax.broadcasted_iota(jnp.int32, (1, PAIR), 1) // (PAIR // 2) == j


def masked_scores(k, qm, toe, length, t, causal):
    scores = dot(k, qm, NT)
    rows = scores.shape[0]
    key = lax.broadcasted_iota(jnp.int32, (rows, TILE), 0)
    if causal:
        bias = toe[:, :TILE]
        if t:
            bias = jnp.concatenate([toe[:, TILE:], bias], axis=0)
        scores = scores + bias
        query = lax.broadcasted_iota(jnp.int32, (rows, TILE), 1) + t * TILE
        allowed = key <= jnp.minimum(query, length - 1)
    else:
        allowed = key < length
    return jnp.where(allowed, scores, NEGATIVE)


def spread(row_ref, toe_ref):
    for j in range(2):
        row = jnp.broadcast_to(row_ref[0, j : j + 1, :], (TILE, 2 * TILE))
        toe_ref[j] = pltpu.roll(row, 0, 1, stride=1, stride_axis=0)


def forward_kernel(causal, len_ref, *refs):
    if causal:
        q_ref, k_ref, v_ref, row_ref, o_ref, lse_ref, toe_ref = refs
    else:
        q_ref, k_ref, v_ref, o_ref, lse_ref = refs
        toe_ref = None
    s = pl.program_id(1)
    length = len_ref[s]
    if causal:

        @pl.when(s == 0)
        def _():
            spread(row_ref, toe_ref)

    q, k, v = q_ref[0], k_ref[0], v_ref[0]
    v_turned = turned(v).astype(jnp.bfloat16)
    cells = [(t, j) for t in range(q.shape[0] // TILE) for j in range(2)]

    def score(t, j):
        seen = (t + 1) * TILE if causal else k.shape[0]
        qm = jnp.where(half_mask(j), q[t * TILE : (t + 1) * TILE], 0)
        return masked_scores(k[:seen], qm, toe_ref[j] if causal else None, length, t, causal)

    outs = []
    ahead = score(*cells[0])
    for i, (t, j) in enumerate(cells):
        scores = ahead
        if i + 1 < len(cells):
            ahead = score(*cells[i + 1])
        here = slice(t * TILE, (t + 1) * TILE)
        top = jnp.max(scores, axis=0, keepdims=True)
        grown = jnp.exp(scores - top)
        total = jnp.sum(grown, axis=0, keepdims=True)
        lse_ref[0, 0, j : j + 1, here] = top + jnp.log(total)
        chances = (grown * (1.0 / total)).astype(jnp.bfloat16)
        outs.append(dot(v_turned[j * 64 : (j + 1) * 64, : scores.shape[0]], chances, NN))
        if j:
            o_ref[0, here, :] = turned(jnp.concatenate(outs, axis=0)).astype(jnp.bfloat16)
            outs = []


def diagonal_sums(v):
    width = v.shape[1]
    groups = v[:8]
    for a in range(8, v.shape[0], 8):
        groups = groups + pltpu.roll(v[a : a + 8], width - a, 1)
    total = groups[:1]
    for b in range(1, 8):
        total = total + pltpu.roll(groups[b : b + 1], width - b, 1)
    return total


def backward_kernel(causal, len_ref, *refs):
    if causal:
        q_ref, k_ref, v_ref, do_ref, lse_ref, row_ref = refs[:6]
        dq_ref, dk_ref, dv_ref, diag_ref, toe_ref, sum_ref = refs[6:]
    else:
        q_ref, k_ref, v_ref, do_ref, lse_ref = refs[:5]
        dq_ref, dk_ref, dv_ref = refs[5:]
        toe_ref = None
    s = pl.program_id(1)
    length = len_ref[s]
    if causal:

        @pl.when(s == 0)
        def _():
            spread(row_ref, toe_ref)
            sum_ref[...] = jnp.zeros_like(sum_ref)

    q, k, v, do = q_ref[0], k_ref[0], v_ref[0], do_ref[0]
    k_turned = turned(k).astype(jnp.bfloat16)
    tiles = q.shape[0] // TILE
    dk = [None] * tiles
    dv = [None] * tiles
    cells = [(t, j) for t in range(tiles) for j in range(2)]
    outs = []

    def add(held, value):
        return value if held is None else held + value

    def score(t, j):
        seen = (t + 1) * TILE if causal else k.shape[0]
        here = slice(t * TILE, (t + 1) * TILE)
        qm = jnp.where(half_mask(j), q[here], 0)
        dom = jnp.where(half_mask(j), do[here], 0)
        scores = masked_scores(k[:seen], qm, toe_ref[j] if causal else None, length, t, causal)
        return scores, dot(v[:seen], dom, NT), qm, dom

    def finish(t, j, chances, d_scores, qm, dom):
        seen = d_scores.shape[0]
        outs.append(dot(k_turned[j * 64 : (j + 1) * 64, :seen], d_scores, NN))
        dv_part = dot(chances, dom, NN)
        dk_part = dot(d_scores, qm, NN)
        for b in range(seen // TILE):
            rows = slice(b * TILE, (b + 1) * TILE)
            dv[b] = add(dv[b], dv_part[rows])
            dk[b] = add(dk[b], dk_part[rows])
        if causal:
            if t:
                sum_ref[j, :, TILE:] += d_scores[: t * TILE].astype(jnp.float32)
            sum_ref[j, :, :TILE] += d_scores[t * TILE :].astype(jnp.float32)
        if j:
            here = slice(t * TILE, (t + 1) * TILE)
            dq_ref[0, here, :] = turned(jnp.concatenate(outs, axis=0)).astype(jnp.bfloat16)
            outs.clear()

    ahead = score(*cells[0])
    behind = None
    for i, (t, j) in enumerate(cells):
        scores, d_chances, qm, dom = ahead
        if i + 1 < len(cells):
            ahead = score(*cells[i + 1])
        here = slice(t * TILE, (t + 1) * TILE)
        chances = jnp.exp(scores - lse_ref[0, 0, j : j + 1, here])
        delta = jnp.sum(chances * d_chances, axis=0, keepdims=True)
        d_scores = (chances * (d_chances - delta)).astype(jnp.bfloat16)
        if behind is not None:
            finish(*behind)
        behind = (t, j, chances.astype(jnp.bfloat16), d_scores, qm, dom)
    finish(*behind)
    for b in range(tiles):
        rows = slice(b * TILE, (b + 1) * TILE)
        dk_ref[0, rows, :] = dk[b].astype(jnp.bfloat16)
        dv_ref[0, rows, :] = dv[b].astype(jnp.bfloat16)
    if causal:

        @pl.when(s == pl.num_programs(1) - 1)
        def _():
            for j in range(2):
                diag_ref[0, j : j + 1, :] = diagonal_sums(sum_ref[j])


def attend(kind, q, k, v, lengths, row=None, do=None, lse=None, waits=()):
    count, slots, width = q.shape
    pairs = width // PAIR
    assert slots == 2 * TILE and k.shape[1] == 2 * TILE
    block = pl.BlockSpec((1, slots, PAIR), lambda p, s: (s, 0, p))
    lse_block = pl.BlockSpec((1, 1, 2, slots), lambda p, s: (s, p, 0, 0))
    row_block = pl.BlockSpec((1, 2, slots), lambda p, s: (p, 0, 0))
    state = jax.ShapeDtypeStruct(q.shape, jnp.bfloat16)
    causal = row is not None
    ins, specs = [lengths, q, k, v], [pl.BlockSpec(memory_space=pltpu.SMEM), block, block, block]
    if kind == "forward":
        body = forward_kernel
        outs = [state, jax.ShapeDtypeStruct((count, pairs, 2, slots), jnp.float32)]
        out_specs = [block, lse_block]
    else:
        body = backward_kernel
        ins += [do, lse]
        specs += [block, lse_block]
        outs = [state] * 3
        out_specs = [block] * 3
    scratch = []
    if causal:
        ins.append(row)
        specs.append(row_block)
        scratch.append(pltpu.VMEM((2, TILE, 2 * TILE), jnp.float32))
        if kind == "backward":
            outs.append(jax.ShapeDtypeStruct(row.shape, jnp.float32))
            out_specs.append(row_block)
            scratch.append(pltpu.VMEM((2, TILE, 2 * TILE), jnp.float32))
    return call(
        functools.partial(body, causal),
        ins,
        outs,
        ("self_" if causal else "cross_") + kind,
        waits,
        specs,
        vmem=24,
        cost=lasting(200),
        grid=(pairs, count),
        out_specs=out_specs,
        scratch_shapes=scratch,
    )


FF_TILE = 256
ROW_TILE = 256


def feed_kernel(n_ref, df_ref, in_ref, out_ref, product_ref, gate_ref, up_ref):
    scale, cubic = 0.7978845608028654, 0.044715

    def dots(r):
        rows = slice(r * ROW_TILE, (r + 1) * ROW_TILE)
        n = n_ref[rows, :]
        return (
            dot(n, in_ref[0], NN),
            dot(n, in_ref[1], NN),
            dot(df_ref[rows, :], out_ref[...], NT),
        )

    count = n_ref.shape[0] // ROW_TILE
    ahead = dots(0)
    for r in range(count):
        gate, up, d_product = ahead
        if r + 1 < count:
            ahead = dots(r + 1)
        rows = slice(r * ROW_TILE, (r + 1) * ROW_TILE)
        square = gate * gate
        bend = jnp.tanh(scale * (gate + cubic * (square * gate)))
        half = 0.5 * (1.0 + bend)
        gelu = gate * half
        slope = half + (0.5 * scale) * gate * (1.0 - bend * bend) * (1.0 + 3 * cubic * square)
        product_ref[rows, :] = (gelu * up).astype(jnp.bfloat16)
        gate_ref[rows, :] = (d_product * up * slope).astype(jnp.bfloat16)
        up_ref[rows, :] = (d_product * gelu).astype(jnp.bfloat16)


def feed(n, df, ffin, ffout):
    count, width = n.shape
    hidden = ffout.shape[0]
    whole = pl.BlockSpec((count, width), lambda i: (0, 0))
    tile = pl.BlockSpec((count, FF_TILE), lambda i: (0, i))
    state = jax.ShapeDtypeStruct((count, hidden), jnp.bfloat16)
    specs = [
        whole,
        whole,
        pl.BlockSpec((2, width, FF_TILE), lambda i: (0, 0, i)),
        pl.BlockSpec((FF_TILE, width), lambda i: (i, 0)),
    ]
    return call(
        feed_kernel,
        [n, df, ffin, ffout],
        [state] * 3,
        "feed",
        (),
        specs,
        cost=lasting(100),
        grid=(hidden // FF_TILE,),
        out_specs=[tile] * 3,
    )


def matmuls_kernel(*refs, count, dims, ends):
    total = dot(refs[0][...], refs[count][0], dims)
    for i in range(1, count):
        total = total + dot(refs[i][...], refs[count + i][0], dims)
    if ends:
        total = (total + refs[2 * count][...]) * refs[2 * count + 1][...]
    refs[-1][...] = total


def matmuls(lefts, weights, dims, name, waits=(), ends=(), cost=FREE):
    lefts = [v.reshape(-1, v.shape[-1]) for v in lefts]
    ends = [v.reshape(-1, v.shape[-1]) for v in ends]
    rows = lefts[0].shape[0]
    width = weights[0][0].shape[1 if dims == NT else 2]

    def tile(v):
        return pl.BlockSpec((ROW_TILE, v.shape[1]), lambda i: (i, 0))

    def layer(v, k):
        return pl.BlockSpec((1,) + v.shape[1:], lambda i: (k, 0, 0))

    out = shape_of((rows, width), jnp.float32)
    return call(
        functools.partial(matmuls_kernel, count=len(lefts), dims=dims, ends=bool(ends)),
        lefts + [w for w, _ in weights] + ends,
        out,
        name,
        waits,
        [tile(v) for v in lefts] + [layer(*w) for w in weights] + [tile(v) for v in ends],
        cost=cost,
        grid=(rows // ROW_TILE,),
        out_specs=tile(out),
    )


def grads_kernel(where_ref, *refs, pairs, lefts, rights):
    left_refs, right_refs = refs[:lefts], refs[lefts : lefts + rights]
    sent_ref, kept_ref = refs[-2:]
    first = where_ref[0] == 0
    for i, left in enumerate(left_refs):
        for m in range(0, left.shape[1], ROW_TILE):
            rows = slice(m, m + ROW_TILE)
            block = turned(left[:, rows]).astype(jnp.bfloat16)
            at = 0
            for k, j in pairs:
                right = right_refs[j]
                w = right.shape[1] // 2
                if k == i:
                    both = dot(block, right[...], NN)
                    near, far = both[:, :w], both[:, w:]
                    sent_ref[rows, at : at + w] = jnp.where(first, far, near).astype(jnp.bfloat16)
                    kept_ref[rows, at : at + w] = jnp.where(first, near, far)
                at += w


def stage_grads(place, lefts, rights, pairs, *waits):
    lefts = [v.reshape(-1, v.shape[-1]) for v in lefts]
    rights = [v.reshape(-1, v.shape[-1]) for v in rights]
    height = lefts[0].shape[1]
    width = sum(rights[j].shape[1] // 2 for _, j in pairs)
    ins = [place.c.reshape(1).astype(jnp.int32)] + lefts + rights
    sent, kept = call(
        functools.partial(
            grads_kernel, pairs=tuple(pairs), lefts=len(lefts), rights=len(rights)
        ),
        ins,
        [shape_of((height, width)), shape_of((height, width), jnp.float32)],
        "grads",
        waits,
        [SMEM] + [VMEM] * (len(ins) - 1),
        vmem=36,
    )
    shape = (place.fsdp, 2, height // place.fsdp // 2, width)
    return Reduce(place, sent.reshape(shape), kept.reshape(shape))


def rms_scale(values, factor):
    return values * lax.rsqrt(jnp.mean(values * values, axis=-1, keepdims=True) + EPS) * factor


def rms_back(values, factor, grad_out):
    return jax.vjp(rms_scale, values, factor)[1](grad_out)


def project(a, w):
    return jnp.einsum("vgq,qy->vgy", a, w, preferred_element_type=jnp.float32)


def project_back(a, w):
    return jnp.einsum("gjr,fr->gjf", a, w, preferred_element_type=jnp.float32)


def bucket_hot(extent, buckets):
    distance = jnp.arange(extent, dtype=jnp.int32)
    far = 16 + sum(((distance >= border).astype(jnp.int32) for border in STEPS))
    bucket = jnp.where(distance < 16, distance, far)
    return (bucket[:, None] == jnp.arange(buckets, dtype=jnp.int32)).astype(jnp.float32)


def per_device(
    rep,
    fsdp,
    tokens,
    encoder_states,
    cotangent,
    qkv_weight,
    out_weight,
    ffin_weight,
    ffout_weight,
    norm_gains,
    bias_table,
    lengths,
    enc_lengths,
):
    place = Place(rep, fsdp)
    seq_len, width = tokens.shape[1:]
    table_rows, heads = bias_table.shape
    shard = qkv_weight.shape[3]
    first = place.c == 0
    half = ffin_weight.shape[3] // 2
    part = width // 2

    small_count = 3 * shard + table_rows * heads
    small = jnp.concatenate([norm_gains.reshape(-1), bias_table.reshape(-1)])
    small = jnp.pad(small, (0, SMALL_ROWS * LANES - small_count)).reshape(SMALL_ROWS, LANES)
    stages = [
        Gather(place, [jnp.concatenate([qkv_weight[0, 0], out_weight[0, :1]])], True, small),
        Gather(place, [jnp.concatenate([qkv_weight[0, 1], out_weight[0, 1:]])], False),
        Gather(place, [ffin_weight[0], ffout_weight], True),
    ]
    for stage in stages:
        stage.first()
    stages[0].second()
    stages[0].send()
    stages[1].second()
    stages[0].turn(stages[1].stack)
    stages[0].third()
    stages[2].second()
    self_w, small = stages[0].whole(stages[2].stack)
    small = small.reshape(fsdp, SMALL_ROWS * LANES)
    gains = small[:, : 3 * shard].reshape(fsdp, 3, shard)
    gains = wide(jnp.transpose(gains, (1, 0, 2)).reshape(3, width))
    table = wide(small[:, 3 * shard : small_count].reshape(fsdp * table_rows, heads))
    hot = bucket_hot(seq_len, fsdp * table_rows)
    row = jnp.einsum("nb,bh->hn", hot, table, precision=lax.Precision.HIGHEST)
    row = row.reshape(heads // 2, 2, seq_len)

    live = wide(jnp.arange(seq_len, dtype=jnp.int32)[None, :] < lengths[:, None])[:, :, None]
    stream = wide(tokens)
    normed_self = low(rms_scale(stream, gains[0]))
    q1, k1, v1 = (low(project(normed_self, self_w[i])) for i in range(3))
    ready = [stages[1].stack, stages[2].stack]
    stages[1].send()
    stages[2].send()
    o1, lse1 = attend("forward", q1, k1, v1, lengths, row, waits=ready)
    stages[1].turn(o1)
    stages[1].third()
    middle = stream + project(o1, self_w[3])
    normed_cross = low(rms_scale(middle, gains[1]))
    cross_w, = stages[1].whole(*stages[1].onward)
    q2 = low(project(normed_cross, cross_w[0]))
    k2, v2 = (low(project(encoder_states, cross_w[i])) for i in (1, 2))
    stages[2].turn(cross_w)
    stages[2].third()
    o2, lse2 = attend("forward", q2, k2, v2, enc_lengths, waits=stages[2].onward)
    later = middle + project(o2, cross_w[3])
    normed_feed = low(rms_scale(later, gains[2]))
    stages[2].settle(o2)
    ffin, ffout = stages[2].whole(o2)

    def flat(v):
        return v.reshape(-1, v.shape[-1])

    grad = wide(cotangent) * live
    grad_low = low(grad)
    product, grad_gate, grad_upward = (
        v.reshape(tokens.shape[:2] + (2 * half,))
        for v in feed(flat(normed_feed), flat(grad_low), ffin, ffout[0])
    )

    ffin_sum = stage_grads(place, [normed_feed], [grad_gate, grad_upward], [(0, 0), (0, 1)])
    ffin_sum.send()
    ffout_sum = stage_grads(place, [product], [grad_low], [(0, 0)], *ffin_sum.sent)
    ffin_sum.step("x", *ffout_sum.sent)
    ffout_sum.send()
    grad_normed = matmuls(
        [grad_gate, grad_upward], [(ffin, 0), (ffin, 1)], NT, "grad_normed", ffin_sum.sent, cost=lasting(100)
    ).reshape(tokens.shape)
    grad_norm, gain_feed = rms_back(later, gains[2], grad_normed)
    grad_later = grad + grad_norm
    ffout_sum.step("y", *ffin_sum.sent)

    da2 = low(grad_later)
    do = low(project_back(da2, cross_w[3]))
    ready = ffout_sum.sent + ffin_sum.sent
    ffin_sum.send()
    ffout_sum.send()
    dq2, dk2, dv2 = attend("backward", q2, k2, v2, enc_lengths, None, do, lse2, ready)
    ffin_sum.step("y", dq2)
    ffout_sum.step("x", *ffin_sum.sent)
    ffin_sum.send()
    ffout_sum.send()
    grad_norm, gain_cross = rms_back(middle, gains[1], project_back(dq2, cross_w[0]))
    grad_middle = grad_later + grad_norm
    da1 = low(grad_middle)
    cross_sum = stage_grads(
        place,
        [normed_cross, encoder_states, o2, o1],
        [dq2, dk2, dv2, da2, da1],
        [(0, 0), (1, 1), (1, 2), (2, 3), (3, 4)],
        *ffout_sum.sent,
    )
    cross_sum.send()
    do = low(project_back(da1, self_w[3]))
    cross_sum.step("y")
    ffin_sum.step("z", *cross_sum.sent)

    ready = cross_sum.sent + ffin_sum.sent
    cross_sum.send()
    ffin_sum.send()
    dq1, dk1, dv1, diagonals = attend("backward", q1, k1, v1, lengths, row, do, lse1, ready)
    self_sum = stage_grads(
        place, [normed_self], [dq1, dk1, dv1], [(0, 0), (0, 1), (0, 2)]
    )
    ffout_sum.step("z", *self_sum.sent)
    cross_sum.step("x", *self_sum.sent)
    ready = self_sum.sent + ffout_sum.sent + cross_sum.sent
    self_sum.send()
    cross_sum.send()
    ffout_sum.send()
    encoder_grad = matmuls(
        [dk2, dv2], [(cross_w, 1), (cross_w, 2)], NT, "encoder_grad", ready, cost=lasting(100)
    ).reshape(tokens.shape)
    self_sum.step("y", encoder_grad)
    self_sum.send()
    into = matmuls(
        [dq1, dk1, dv1],
        [(self_w, 0), (self_w, 1), (self_w, 2)],
        NT,
        "into",
        self_sum.sent,
        cost=lasting(200),
    ).reshape(tokens.shape)
    grad_norm, gain_self = rms_back(stream, gains[0], into)
    token_grad = grad_middle + grad_norm
    cross_sum.step("z", into)
    cross_sum.send()
    output_state = matmuls(
        [product],
        [(ffout, 0)],
        NN,
        "output_state",
        cross_sum.sent,
        [later, jnp.broadcast_to(live, tokens.shape[:2] + (1,))],
    ).reshape(tokens.shape)
    self_sum.step("x", output_state)
    self_sum.send()
    ffin_sum.finish(*self_sum.sent)
    ffout_sum.finish(*self_sum.sent)
    grad_table = jnp.einsum(
        "nb,hn->bh", hot, diagonals.reshape(heads, seq_len), precision=lax.Precision.HIGHEST
    )
    small = jnp.stack([gain_self, gain_cross, gain_feed]).reshape(3, fsdp, shard)
    small = jnp.concatenate(
        [
            jnp.transpose(small, (1, 0, 2)).reshape(fsdp, 3 * shard),
            grad_table.reshape(fsdp, table_rows * heads),
        ],
        axis=1,
    )
    small = held_back(jnp.pad(small, ((0, 0), (0, -small_count % 128))), self_sum.sent)
    small = reduce_small(place, small)
    self_sum.step("z")
    self_sum.send()
    cross_sum.finish(*self_sum.sent)
    self_sum.finish()

    def matrices(stage, size):
        near, far = stage.done()
        return [
            jnp.concatenate([near[:, i : i + size], far[:, i : i + size]], axis=1)
            for i in range(0, near.shape[1], size)
        ]

    cross_grads = matrices(cross_sum, part)
    self_grads = matrices(self_sum, part)
    qkv_grad = jnp.stack([jnp.stack(self_grads), jnp.stack(cross_grads[:3])])[None]
    out_grad = jnp.stack([cross_grads[4], cross_grads[3]])[None]
    ffin_grad = jnp.stack(matrices(ffin_sum, half))[None]
    ffout_grad = matrices(ffout_sum, part)[0][None]
    return (
        output_state,
        token_grad,
        encoder_grad,
        qkv_grad,
        out_grad,
        ffin_grad,
        ffout_grad,
        small[: 3 * shard].reshape(1, 3, shard),
        small[3 * shard : small_count].reshape(table_rows, heads),
    )


def solution(mesh):
    in_specs = (
        P(("rep", "fsdp"), None, None),
        P(("rep", "fsdp"), None, None),
        P(("rep", "fsdp"), None, None),
        P(None, None, None, "fsdp", None),
        P(None, None, "fsdp", None),
        P(None, None, "fsdp", None),
        P(None, "fsdp", None),
        P(None, None, "fsdp"),
        P("fsdp", None),
        P(("rep", "fsdp")),
        P(("rep", "fsdp")),
    )
    out_specs = (
        P(("rep", "fsdp"), None, None),
        P(("rep", "fsdp"), None, None),
        P(("rep", "fsdp"), None, None),
        P(None, None, None, "fsdp", None),
        P(None, None, "fsdp", None),
        P(None, None, "fsdp", None),
        P(None, "fsdp", None),
        P(None, None, "fsdp"),
        P("fsdp", None),
    )
    return jax.shard_map(
        functools.partial(per_device, mesh.shape["rep"], mesh.shape["fsdp"]),
        mesh=mesh, in_specs=in_specs, out_specs=out_specs, check_vma=False
    )
```

```python
import functools

import jax
import jax.numpy as jnp
from jax import lax
from jax.experimental import pallas as pl
from jax.experimental.pallas import tpu as pltpu
from jax.sharding import PartitionSpec as P

EPS = 1e-06
STEPS = (19, 21, 24, 27, 31, 35, 40, 46, 52, 59, 67, 77, 87, 99, 113)


Z = 4


class Place:
    def __init__(self, rep, fsdp):
        self.rep, self.fsdp = rep, fsdp
        self.nx = fsdp // Z
        r = lax.axis_index("rep")
        f = lax.axis_index("fsdp")
        self.c, self.y = r % 2, (r // 2) % 2
        self.z, self.x = f // self.nx, f % self.nx
        self.q = 2 * self.y + self.c

    def core(self, v):
        return lax.ppermute(v, "rep", [(i, i ^ 1) for i in range(self.rep)])

    def across(self, v, bit):
        return lax.ppermute(v, "rep", [(i, i ^ bit) for i in range(self.rep)])

    def along_x(self, v, d):
        nx = self.nx
        return lax.ppermute(
            v, "fsdp", [(i, i // nx * nx + (i % nx + d) % nx) for i in range(self.fsdp)]
        )

    def along_z(self, v, d):
        return lax.ppermute(
            v, "fsdp", [(i, (i + d * self.nx) % self.fsdp) for i in range(self.fsdp)]
        )


def low(v):
    return v.astype(jnp.bfloat16)


def wide(v):
    return v.astype(jnp.float32)


def pick(v, i, axis=0):
    return lax.dynamic_index_in_dim(v, i, axis, keepdims=False)


FREE = pl.CostEstimate(flops=0, bytes_accessed=0, transcendentals=0)


def lasting(microseconds):
    return pl.CostEstimate(
        flops=int(microseconds * 1e9), bytes_accessed=0, transcendentals=0
    )


VMEM = pl.BlockSpec(memory_space=pltpu.VMEM)
SMEM = pl.BlockSpec(memory_space=pltpu.SMEM)


def shape_of(shape, dtype=jnp.bfloat16):
    return jax.ShapeDtypeStruct(shape, dtype)


def call(body, ins, outs, name, waits=(), specs=None, vmem=32, cost=FREE, **kw):
    waits = list(waits)
    count, late = len(ins), len(ins) + len(waits)

    def kernel(*refs):
        body(*refs[:count], *refs[late:])

    return pl.pallas_call(
        kernel,
        in_specs=list(specs or [VMEM] * count) + [pl.BlockSpec(memory_space=pl.ANY)] * len(waits),
        out_shape=outs,
        name=name,
        compiler_params=pltpu.CompilerParams(vmem_limit_bytes=vmem * 1024 * 1024),
        cost_estimate=cost,
        **kw,
    )(*ins, *waits)


def stack_kernel(*refs):
    for k, ref in enumerate(refs[:-1]):
        refs[-1][k] = ref[...]


def copy_kernel(ref, out):
    out[...] = ref[...]


def stacked(values, waits=()):
    shape = shape_of((len(values),) + values[0].shape, values[0].dtype)
    return call(stack_kernel, values, shape, "stack", waits)


def held_back(value, waits):
    return call(copy_kernel, [value], shape_of(value.shape, value.dtype), "hold", waits)


LANES = 128
SMALL_ROWS = 16


def assemble_kernel(where_ref, *refs, parts, nx, sizes, small):
    outs = refs[len(parts) :]
    c, y, z, x = (where_ref[i] for i in range(4))
    for ref, (dc, dy, dx) in zip(refs, parts):
        core = c ^ dc
        row = y ^ dy
        col = lax.rem(x - dx + nx, nx)
        for k in range(Z):
            f = lax.rem(z - k + Z, Z) * nx + col
            at = 0
            for out, (m, h, w) in zip(outs, sizes):
                for t in range(w // LANES):
                    lane = pl.ds(pl.multiple_of(core * w + t * LANES, LANES), LANES)
                    for i in range(m):
                        out[i, f, row, :, lane] = ref[k, at : at + h, :]
                        at += h
            if small and (dc, dy) == (0, 0):
                outs[-1][f] = ref[k, at : at + SMALL_ROWS, :]


class Gather:
    def __init__(self, place, shards, y_last, small=None):
        self.place, self.y_last, self.small = place, y_last, small
        self.sizes, rows = [], []
        for shard in shards:
            m, h, w = shard.shape[0], shard.shape[1] // 2, shard.shape[2] // 2
            self.sizes.append((m, h, w))
            cut = lax.dynamic_slice(shard, (0, place.y * h, place.c * w), (m, h, w))
            cut = jnp.transpose(cut.reshape(m, h, w // LANES, LANES), (2, 0, 1, 3))
            rows.append(cut.reshape(-1, LANES))
        if small is not None:
            rows.append(small)
        self.piece = rows[0] if len(rows) == 1 else jnp.concatenate(rows)

    def first(self):
        self.pieces = [self.piece] + [self.place.along_z(self.piece, d) for d in range(1, Z)]

    def second(self, *waits):
        self.stack = stacked(self.pieces, waits)

    def send(self):
        place, stack = self.place, self.stack
        self.held = {(0, 0): stack}
        for d in range(1, place.nx):
            self.held[0, d] = place.along_x(stack, d)
        self.held[1, 0] = place.across(stack, 2)

    def turn(self, *waits):
        self.onward = []
        for d in range(1, self.place.nx) if self.y_last else (0,):
            key = (0, d) if self.y_last else (1, 0)
            if waits:
                self.held[key] = held_back(self.held[key], waits)
            self.onward.append(self.held[key])

    def third(self):
        place, nx = self.place, self.place.nx
        for d in range(1, nx):
            if self.y_last:
                self.held[1, d] = place.across(self.held[0, d], 2)
            else:
                self.held[1, d] = place.along_x(self.held[1, 0], d)

    def settle(self, *waits):
        for d in range(1, self.place.nx):
            self.held[1, d] = held_back(self.held[1, d], waits)

    def whole(self, *waits):
        place = self.place
        parts, arrays = [], []
        for key, value in self.held.items():
            parts += [(0,) + key, (1,) + key]
            arrays += [value, place.across(value, 1)]
        shapes = [shape_of((m, place.fsdp, 2, h, 2 * w)) for m, h, w in self.sizes]
        if self.small is not None:
            shapes.append(shape_of((place.fsdp, SMALL_ROWS, LANES)))
        where = jnp.stack([place.c, place.y, place.z, place.x]).astype(jnp.int32)
        body = functools.partial(
            assemble_kernel,
            parts=tuple(parts),
            nx=place.nx,
            sizes=tuple(self.sizes),
            small=self.small is not None,
        )
        specs = [SMEM] + [VMEM] * len(arrays)
        full = call(body, [where] + arrays, shapes, "assemble", waits, specs, vmem=36)
        whole = [
            v.reshape(m, place.fsdp * 2 * h, 2 * w) for v, (m, h, w) in zip(full, self.sizes)
        ]
        return whole + list(full[len(whole) :])


def step_kernel(where_ref, kept_ref, *refs, axis, count, lead):
    got, keep_ref, send_refs = refs[: -count], refs[-count], refs[len(refs) - count + 1 :]
    own = where_ref[0]
    rest = [()]
    for size in lead[:axis] + lead[axis + 1 :]:
        rest = [r + (i,) for r in rest for i in range(size)]

    def value(at):
        total = kept_ref[at]
        for ref in got:
            total = total + ref[at].astype(jnp.float32)
        return total

    for r in rest:
        keep_ref[r] = value(r[:axis] + (own,) + r[axis:])
        for d, ref in enumerate(send_refs, 1):
            there = lax.rem(own + d, count)
            ref[r] = value(r[:axis] + (there,) + r[axis:]).astype(jnp.bfloat16)


def total_kernel(kept_ref, *refs):
    total = kept_ref[...]
    for ref in refs[:-1]:
        total = total + ref[...].astype(jnp.float32)
    refs[-1][...] = total


def rows_kernel(where_ref, total_ref, other_ref, out):
    h = total_ref.shape[0]
    y = where_ref[0]
    out[pl.ds(pl.multiple_of(y * h, 8), h), :] = total_ref[...]
    out[pl.ds(pl.multiple_of((1 - y) * h, 8), h), :] = other_ref[...]


class Reduce:
    def __init__(self, place, sent, kept):
        self.place = place
        lead = (Z, place.nx, 2)
        self.sent = [sent]
        self.kept = kept.reshape(lead + kept.shape[2:])
        self.axes = ["z", "x", "y"]
        self.name = "core"

    def send(self):
        place = self.place
        if self.name == "core":
            self.got = [place.across(self.sent[0], 1).reshape(self.kept.shape)]
        elif self.name == "y":
            self.got = [place.across(self.sent[0], 2)]
        else:
            move = place.along_x if self.name == "x" else place.along_z
            self.got = [move(v, d) for d, v in enumerate(self.sent, 1)]

    def step(self, name, *waits, cost=FREE):
        place = self.place
        axis = self.axes.index(name)
        lead, tail = self.kept.shape[:-2], self.kept.shape[-2:]
        count = lead[axis]
        left = lead[:axis] + lead[axis + 1 :] + tail
        own = {"z": place.z, "x": place.x, "y": place.y}[name].reshape(1).astype(jnp.int32)
        outs = [shape_of(left, jnp.float32)] + [shape_of(left)] * (count - 1)
        body = functools.partial(step_kernel, axis=axis, count=count, lead=lead)
        ins = [own, self.kept] + self.got
        specs = [SMEM] + [VMEM] * (len(ins) - 1)
        self.kept, *self.sent = call(
            body, ins, outs, "step_" + name, waits, specs, cost=cost
        )
        self.axes.remove(name)
        self.name = name

    def finish(self, *waits, cost=FREE):
        place = self.place
        shape = shape_of(self.kept.shape, jnp.float32)
        total = call(total_kernel, [self.kept] + self.got, shape, "total", waits, cost=cost)
        bit = 4
        while bit < place.rep:
            total = total + place.across(total, bit)
            bit *= 2
        self.total, self.other = total, place.across(total, 2)

    def rows(self, *waits, cost=FREE):
        place = self.place
        h, w = self.total.shape
        ins = [place.y.reshape(1).astype(jnp.int32), self.total, self.other]
        out = shape_of((2 * h, w), jnp.float32)
        self.near = call(rows_kernel, ins, out, "rows", waits, [SMEM, VMEM, VMEM], cost=cost)
        self.far = place.across(self.near, 1)

    def done(self):
        first = self.place.c == 0
        return jnp.where(first, self.near, self.far), jnp.where(first, self.far, self.near)


def sum_replicas(place, partial):
    bit = 1
    while bit < place.rep:
        partial = partial + place.across(partial, bit)
        bit *= 2
    return partial


def sum_owners(place, partial):
    total = partial.reshape(Z, place.nx, -1)
    near = pick(total, place.x, 1)
    for d in range(1, place.nx):
        near = near + place.along_x(pick(total, (place.x + d) % place.nx, 1), d)
    mine = pick(near, place.z)
    for d in range(1, Z):
        mine = mine + place.along_z(pick(near, (place.z + d) % Z), d)
    return mine


NEGATIVE = -1e30
TILE = 256
PAIR = 128


def dot(a, b, dims):
    return lax.dot_general(a, b, (dims, ((), ())), preferred_element_type=jnp.float32)


NT = ((1,), (1,))
NN = ((1,), (0,))
TN = ((0,), (0,))


def turned(v):
    return v.astype(jnp.float32).T


def half_mask(j):
    return lax.broadcasted_iota(jnp.int32, (1, PAIR), 1) // (PAIR // 2) == j


def masked_scores(k, qm, toe, length, t, causal):
    scores = dot(k, qm, NT)
    rows = scores.shape[0]
    key = lax.broadcasted_iota(jnp.int32, (rows, TILE), 0)
    if causal:
        bias = toe[:, :TILE]
        if t:
            bias = jnp.concatenate([toe[:, TILE:], bias], axis=0)
        scores = scores + bias
        query = lax.broadcasted_iota(jnp.int32, (rows, TILE), 1) + t * TILE
        allowed = key <= jnp.minimum(query, length - 1)
    else:
        allowed = key < length
    return jnp.where(allowed, scores, NEGATIVE)


def spread(row_ref, toe_ref):
    for j in range(2):
        row = jnp.broadcast_to(row_ref[0, j : j + 1, :], (TILE, 2 * TILE))
        toe_ref[j] = pltpu.roll(row, 0, 1, stride=1, stride_axis=0)


def forward_kernel(causal, len_ref, *refs):
    if causal:
        q_ref, k_ref, v_ref, row_ref, o_ref, lse_ref, toe_ref = refs
    else:
        q_ref, k_ref, v_ref, o_ref, lse_ref = refs
        toe_ref = None
    s = pl.program_id(1)
    length = len_ref[s]
    if causal:

        @pl.when(s == 0)
        def _():
            spread(row_ref, toe_ref)

    q, k, v = q_ref[0], k_ref[0], v_ref[0]
    v_turned = turned(v).astype(jnp.bfloat16)
    cells = [(t, j) for t in range(q.shape[0] // TILE) for j in range(2)]

    def score(t, j):
        seen = (t + 1) * TILE if causal else k.shape[0]
        qm = jnp.where(half_mask(j), q[t * TILE : (t + 1) * TILE], 0)
        return masked_scores(k[:seen], qm, toe_ref[j] if causal else None, length, t, causal)

    outs = []
    ahead = score(*cells[0])
    for i, (t, j) in enumerate(cells):
        scores = ahead
        if i + 1 < len(cells):
            ahead = score(*cells[i + 1])
        here = slice(t * TILE, (t + 1) * TILE)
        top = jnp.max(scores, axis=0, keepdims=True)
        grown = jnp.exp(scores - top)
        total = jnp.sum(grown, axis=0, keepdims=True)
        lse_ref[0, 0, j : j + 1, here] = top + jnp.log(total)
        chances = (grown * (1.0 / total)).astype(jnp.bfloat16)
        outs.append(dot(v_turned[j * 64 : (j + 1) * 64, : scores.shape[0]], chances, NN))
        if j:
            o_ref[0, here, :] = turned(jnp.concatenate(outs, axis=0)).astype(jnp.bfloat16)
            outs = []


def diagonal_sums(v):
    width = v.shape[1]
    groups = v[:8]
    for a in range(8, v.shape[0], 8):
        groups = groups + pltpu.roll(v[a : a + 8], width - a, 1)
    total = groups[:1]
    for b in range(1, 8):
        total = total + pltpu.roll(groups[b : b + 1], width - b, 1)
    return total


def backward_kernel(causal, len_ref, *refs):
    if causal:
        q_ref, k_ref, v_ref, do_ref, lse_ref, row_ref = refs[:6]
        dq_ref, dk_ref, dv_ref, diag_ref, toe_ref, sum_ref = refs[6:]
    else:
        q_ref, k_ref, v_ref, do_ref, lse_ref = refs[:5]
        dq_ref, dk_ref, dv_ref = refs[5:]
        toe_ref = None
    s = pl.program_id(1)
    length = len_ref[s]
    if causal:

        @pl.when(s == 0)
        def _():
            spread(row_ref, toe_ref)
            sum_ref[...] = jnp.zeros_like(sum_ref)

    q, k, v, do = q_ref[0], k_ref[0], v_ref[0], do_ref[0]
    k_turned = turned(k).astype(jnp.bfloat16)
    tiles = q.shape[0] // TILE
    dk = [None] * tiles
    dv = [None] * tiles
    cells = [(t, j) for t in range(tiles) for j in range(2)]
    outs = []

    def add(held, value):
        return value if held is None else held + value

    def score(t, j):
        seen = (t + 1) * TILE if causal else k.shape[0]
        here = slice(t * TILE, (t + 1) * TILE)
        qm = jnp.where(half_mask(j), q[here], 0)
        dom = jnp.where(half_mask(j), do[here], 0)
        scores = masked_scores(k[:seen], qm, toe_ref[j] if causal else None, length, t, causal)
        return scores, dot(v[:seen], dom, NT), qm, dom

    def finish(t, j, chances, d_scores, qm, dom):
        seen = d_scores.shape[0]
        outs.append(dot(k_turned[j * 64 : (j + 1) * 64, :seen], d_scores, NN))
        dv_part = dot(chances, dom, NN)
        dk_part = dot(d_scores, qm, NN)
        for b in range(seen // TILE):
            rows = slice(b * TILE, (b + 1) * TILE)
            dv[b] = add(dv[b], dv_part[rows])
            dk[b] = add(dk[b], dk_part[rows])
        if causal:
            if t:
                sum_ref[j, :, TILE:] += d_scores[: t * TILE].astype(jnp.float32)
            sum_ref[j, :, :TILE] += d_scores[t * TILE :].astype(jnp.float32)
        if j:
            here = slice(t * TILE, (t + 1) * TILE)
            dq_ref[0, here, :] = turned(jnp.concatenate(outs, axis=0)).astype(jnp.bfloat16)
            outs.clear()

    ahead = score(*cells[0])
    behind = None
    for i, (t, j) in enumerate(cells):
        scores, d_chances, qm, dom = ahead
        if i + 1 < len(cells):
            ahead = score(*cells[i + 1])
        here = slice(t * TILE, (t + 1) * TILE)
        chances = jnp.exp(scores - lse_ref[0, 0, j : j + 1, here])
        delta = jnp.sum(chances * d_chances, axis=0, keepdims=True)
        d_scores = (chances * (d_chances - delta)).astype(jnp.bfloat16)
        if behind is not None:
            finish(*behind)
        behind = (t, j, chances.astype(jnp.bfloat16), d_scores, qm, dom)
    finish(*behind)
    for b in range(tiles):
        rows = slice(b * TILE, (b + 1) * TILE)
        dk_ref[0, rows, :] = dk[b].astype(jnp.bfloat16)
        dv_ref[0, rows, :] = dv[b].astype(jnp.bfloat16)
    if causal:

        @pl.when(s == pl.num_programs(1) - 1)
        def _():
            for j in range(2):
                diag_ref[0, j : j + 1, :] = diagonal_sums(sum_ref[j])


def attend(kind, q, k, v, lengths, row=None, do=None, lse=None, waits=()):
    count, slots, width = q.shape
    pairs = width // PAIR
    assert slots == 2 * TILE and k.shape[1] == 2 * TILE
    block = pl.BlockSpec((1, slots, PAIR), lambda p, s: (s, 0, p))
    lse_block = pl.BlockSpec((1, 1, 2, slots), lambda p, s: (s, p, 0, 0))
    row_block = pl.BlockSpec((1, 2, slots), lambda p, s: (p, 0, 0))
    state = jax.ShapeDtypeStruct(q.shape, jnp.bfloat16)
    causal = row is not None
    ins, specs = [lengths, q, k, v], [pl.BlockSpec(memory_space=pltpu.SMEM), block, block, block]
    if kind == "forward":
        body = forward_kernel
        outs = [state, jax.ShapeDtypeStruct((count, pairs, 2, slots), jnp.float32)]
        out_specs = [block, lse_block]
    else:
        body = backward_kernel
        ins += [do, lse]
        specs += [block, lse_block]
        outs = [state] * 3
        out_specs = [block] * 3
    scratch = []
    if causal:
        ins.append(row)
        specs.append(row_block)
        scratch.append(pltpu.VMEM((2, TILE, 2 * TILE), jnp.float32))
        if kind == "backward":
            outs.append(jax.ShapeDtypeStruct(row.shape, jnp.float32))
            out_specs.append(row_block)
            scratch.append(pltpu.VMEM((2, TILE, 2 * TILE), jnp.float32))
    return call(
        functools.partial(body, causal),
        ins,
        outs,
        ("self_" if causal else "cross_") + kind,
        waits,
        specs,
        vmem=24,
        cost=lasting(200),
        grid=(pairs, count),
        out_specs=out_specs,
        scratch_shapes=scratch,
    )


FF_TILE = 256
ROW_TILE = 256


def feed_kernel(n_ref, df_ref, in_ref, out_ref, product_ref, gate_ref, up_ref):
    scale, cubic = 0.7978845608028654, 0.044715

    def dots(r):
        rows = slice(r * ROW_TILE, (r + 1) * ROW_TILE)
        n = n_ref[rows, :]
        return (
            dot(n, in_ref[0], NN),
            dot(n, in_ref[1], NN),
            dot(df_ref[rows, :], out_ref[...], NT),
        )

    count = n_ref.shape[0] // ROW_TILE
    ahead = dots(0)
    for r in range(count):
        gate, up, d_product = ahead
        if r + 1 < count:
            ahead = dots(r + 1)
        rows = slice(r * ROW_TILE, (r + 1) * ROW_TILE)
        square = gate * gate
        bend = jnp.tanh(scale * (gate + cubic * (square * gate)))
        half = 0.5 * (1.0 + bend)
        gelu = gate * half
        slope = half + (0.5 * scale) * gate * (1.0 - bend * bend) * (1.0 + 3 * cubic * square)
        product_ref[rows, :] = (gelu * up).astype(jnp.bfloat16)
        gate_ref[rows, :] = (d_product * up * slope).astype(jnp.bfloat16)
        up_ref[rows, :] = (d_product * gelu).astype(jnp.bfloat16)


def feed(n, df, ffin, ffout):
    count, width = n.shape
    hidden = ffout.shape[0]
    whole = pl.BlockSpec((count, width), lambda i: (0, 0))
    tile = pl.BlockSpec((count, FF_TILE), lambda i: (0, i))
    state = jax.ShapeDtypeStruct((count, hidden), jnp.bfloat16)
    specs = [
        whole,
        whole,
        pl.BlockSpec((2, width, FF_TILE), lambda i: (0, 0, i)),
        pl.BlockSpec((FF_TILE, width), lambda i: (i, 0)),
    ]
    return call(
        feed_kernel,
        [n, df, ffin, ffout],
        [state] * 3,
        "feed",
        (),
        specs,
        cost=lasting(100),
        grid=(hidden // FF_TILE,),
        out_specs=[tile] * 3,
    )


def matmuls_kernel(*refs, count, dims, ends):
    total = dot(refs[0][...], refs[count][0], dims)
    for i in range(1, count):
        total = total + dot(refs[i][...], refs[count + i][0], dims)
    if ends:
        total = (total + refs[2 * count][...]) * refs[2 * count + 1][...]
    refs[-1][...] = total.astype(refs[-1].dtype)


def matmuls(lefts, weights, dims, name, waits=(), ends=(), cost=FREE, dtype=jnp.float32):
    lefts = [v.reshape(-1, v.shape[-1]) for v in lefts]
    ends = [v.reshape(-1, v.shape[-1]) for v in ends]
    rows = lefts[0].shape[0]
    width = weights[0][0].shape[1 if dims == NT else 2]

    def tile(v):
        return pl.BlockSpec((ROW_TILE, v.shape[1]), lambda i: (i, 0))

    def layer(v, k):
        return pl.BlockSpec((1,) + v.shape[1:], lambda i: (k, 0, 0))

    out = shape_of((rows, width), dtype)
    return call(
        functools.partial(matmuls_kernel, count=len(lefts), dims=dims, ends=bool(ends)),
        lefts + [w for w, _ in weights] + ends,
        out,
        name,
        waits,
        [tile(v) for v in lefts] + [layer(*w) for w in weights] + [tile(v) for v in ends],
        cost=cost,
        grid=(rows // ROW_TILE,),
        out_specs=tile(out),
    )


def grads_kernel(where_ref, *refs, pairs, lefts, rights):
    left_refs, right_refs = refs[:lefts], refs[lefts : lefts + rights]
    sent_ref, kept_ref = refs[-2:]
    first = where_ref[0] == 0
    for i, left in enumerate(left_refs):
        for m in range(0, left.shape[1], ROW_TILE):
            rows = slice(m, m + ROW_TILE)
            block = turned(left[:, rows]).astype(jnp.bfloat16)
            at = 0
            for k, j in pairs:
                right = right_refs[j]
                w = right.shape[1] // 2
                if k == i:
                    both = dot(block, right[...], NN)
                    near, far = both[:, :w], both[:, w:]
                    sent_ref[rows, at : at + w] = jnp.where(first, far, near).astype(jnp.bfloat16)
                    kept_ref[rows, at : at + w] = jnp.where(first, near, far)
                at += w


def stage_grads(place, lefts, rights, pairs, *waits, cost=FREE):
    lefts = [v.reshape(-1, v.shape[-1]) for v in lefts]
    rights = [v.reshape(-1, v.shape[-1]) for v in rights]
    height = lefts[0].shape[1]
    width = sum(rights[j].shape[1] // 2 for _, j in pairs)
    ins = [place.c.reshape(1).astype(jnp.int32)] + lefts + rights
    sent, kept = call(
        functools.partial(
            grads_kernel, pairs=tuple(pairs), lefts=len(lefts), rights=len(rights)
        ),
        ins,
        [shape_of((height, width)), shape_of((height, width), jnp.float32)],
        "grads",
        waits,
        [SMEM] + [VMEM] * (len(ins) - 1),
        vmem=36,
        cost=cost,
    )
    shape = (place.fsdp, 2, height // place.fsdp // 2, width)
    return Reduce(place, sent.reshape(shape), kept.reshape(shape))


def rms_scale(values, factor):
    return values * lax.rsqrt(jnp.mean(values * values, axis=-1, keepdims=True) + EPS) * factor


def rms_back(values, factor, grad_out):
    return jax.vjp(rms_scale, values, factor)[1](grad_out)


def project(a, w):
    return jnp.einsum("vgq,qy->vgy", a, w, preferred_element_type=jnp.float32)


def project_back(a, w):
    return jnp.einsum("gjr,fr->gjf", a, w, preferred_element_type=jnp.float32)


def bucket_hot(extent, buckets):
    distance = jnp.arange(extent, dtype=jnp.int32)
    far = 16 + sum(((distance >= border).astype(jnp.int32) for border in STEPS))
    bucket = jnp.where(distance < 16, distance, far)
    return (bucket[:, None] == jnp.arange(buckets, dtype=jnp.int32)).astype(jnp.float32)


def per_device(
    rep,
    fsdp,
    tokens,
    encoder_states,
    cotangent,
    qkv_weight,
    out_weight,
    ffin_weight,
    ffout_weight,
    norm_gains,
    bias_table,
    lengths,
    enc_lengths,
):
    place = Place(rep, fsdp)
    seq_len, width = tokens.shape[1:]
    table_rows, heads = bias_table.shape
    shard = qkv_weight.shape[3]
    first = place.c == 0
    half = ffin_weight.shape[3] // 2
    part = width // 2

    small_count = 3 * shard + table_rows * heads
    small = jnp.concatenate([norm_gains.reshape(-1), bias_table.reshape(-1)])
    small = jnp.pad(small, (0, SMALL_ROWS * LANES - small_count)).reshape(SMALL_ROWS, LANES)
    stages = [
        Gather(place, [jnp.concatenate([qkv_weight[0, 0], out_weight[0, :1]])], True, small),
        Gather(place, [jnp.concatenate([qkv_weight[0, 1], out_weight[0, 1:]])], False),
        Gather(place, [ffin_weight[0], ffout_weight], True),
    ]
    for stage in stages:
        stage.first()
    stages[0].second()
    stages[0].send()
    stages[1].second()
    stages[0].turn(stages[1].stack, stages[0].held[1, 0])
    stages[0].third()
    stages[2].second()
    self_w, small = stages[0].whole(stages[2].stack)
    small = small.reshape(fsdp, SMALL_ROWS * LANES)
    gains = small[:, : 3 * shard].reshape(fsdp, 3, shard)
    gains = wide(jnp.transpose(gains, (1, 0, 2)).reshape(3, width))
    table = wide(small[:, 3 * shard : small_count].reshape(fsdp * table_rows, heads))
    hot = bucket_hot(seq_len, fsdp * table_rows)
    row = jnp.einsum("nb,bh->hn", hot, table, precision=lax.Precision.HIGHEST)
    row = row.reshape(heads // 2, 2, seq_len)

    live = wide(jnp.arange(seq_len, dtype=jnp.int32)[None, :] < lengths[:, None])[:, :, None]
    stream = wide(tokens)
    normed_self = low(rms_scale(stream, gains[0]))
    q1, k1, v1 = (low(project(normed_self, self_w[i])) for i in range(3))
    stages[1].send()
    stages[1].turn(self_w)
    stages[1].third()
    stages[2].send()
    ready = stages[1].onward + [stages[2].stack]
    o1, lse1 = attend("forward", q1, k1, v1, lengths, row, waits=ready)
    middle = stream + project(o1, self_w[3])
    normed_cross = low(rms_scale(middle, gains[1]))
    cross_w, = stages[1].whole(o1)
    q2 = low(project(normed_cross, cross_w[0]))
    k2, v2 = (low(project(encoder_states, cross_w[i])) for i in (1, 2))
    stages[2].turn(cross_w)
    stages[2].third()
    o2, lse2 = attend("forward", q2, k2, v2, enc_lengths, waits=stages[2].onward)
    later = middle + project(o2, cross_w[3])
    normed_feed = low(rms_scale(later, gains[2]))
    stages[2].settle(o2)
    ffin, ffout = stages[2].whole(o2)

    def flat(v):
        return v.reshape(-1, v.shape[-1])

    grad = wide(cotangent) * live
    grad_low = low(grad)
    product, grad_gate, grad_upward = (
        v.reshape(tokens.shape[:2] + (2 * half,))
        for v in feed(flat(normed_feed), flat(grad_low), ffin, ffout[0])
    )

    ffin_sum = stage_grads(place, [normed_feed], [grad_gate, grad_upward], [(0, 0), (0, 1)])
    ffin_sum.send()
    ffout_sum = stage_grads(place, [product], [grad_low], [(0, 0)], *ffin_sum.sent)
    ffin_sum.step("x", *ffout_sum.sent)
    ffout_sum.send()
    grad_normed = matmuls(
        [grad_gate, grad_upward], [(ffin, 0), (ffin, 1)], NT, "grad_normed", ffin_sum.sent, cost=lasting(100)
    ).reshape(tokens.shape)
    grad_norm, gain_feed = rms_back(later, gains[2], grad_normed)
    grad_later = grad + grad_norm
    ffout_sum.step("y", *ffin_sum.sent)

    da2 = low(grad_later)
    do = low(project_back(da2, cross_w[3]))
    ready = ffout_sum.sent + ffin_sum.sent
    ffin_sum.send()
    ffout_sum.send()
    dq2, dk2, dv2 = attend("backward", q2, k2, v2, enc_lengths, None, do, lse2, ready)
    ffin_sum.step("y", dq2)
    ffout_sum.step("x", *ffin_sum.sent)
    ffin_sum.send()
    ffout_sum.send()
    grad_norm, gain_cross = rms_back(middle, gains[1], project_back(dq2, cross_w[0]))
    grad_middle = grad_later + grad_norm
    da1 = low(grad_middle)
    cross_sum = stage_grads(
        place,
        [normed_cross, encoder_states, o2, o1],
        [dq2, dk2, dv2, da2, da1],
        [(0, 0), (1, 1), (1, 2), (2, 3), (3, 4)],
        *ffout_sum.sent,
        cost=lasting(100),
    )
    cross_sum.send()
    ffin_sum.step("z", *cross_sum.sent)
    do = matmuls(
        [da1],
        [(self_w, 3)],
        NT,
        "self_do",
        ffin_sum.sent,
        cost=lasting(100),
        dtype=jnp.bfloat16,
    ).reshape(tokens.shape)
    cross_sum.step("y", do)

    ready = cross_sum.sent + ffin_sum.sent
    cross_sum.send()
    ffin_sum.send()
    dq1, dk1, dv1, diagonals = attend("backward", q1, k1, v1, lengths, row, do, lse1, ready)
    ffin_sum.finish(dq1)
    cross_sum.step("x", ffin_sum.total)
    cross_sum.send()
    self_sum = stage_grads(
        place, [normed_self], [dq1, dk1, dv1], [(0, 0), (0, 1), (0, 2)], *cross_sum.sent
    )
    self_sum.send()
    ffout_sum.step("z", *self_sum.sent, cost=lasting(100))
    ffout_sum.send()
    self_sum.step("y", *ffout_sum.sent)
    self_sum.send()
    encoder_grad = matmuls(
        [dk2, dv2],
        [(cross_w, 1), (cross_w, 2)],
        NT,
        "encoder_grad",
        self_sum.sent,
        cost=lasting(100),
    ).reshape(tokens.shape)
    into = matmuls(
        [dq1, dk1, dv1],
        [(self_w, 0), (self_w, 1), (self_w, 2)],
        NT,
        "into",
        [encoder_grad],
    ).reshape(tokens.shape)
    cross_sum.step("z", into)
    cross_sum.send()
    self_sum.step("x", *cross_sum.sent)
    self_sum.send()
    grad_norm, gain_self = rms_back(stream, gains[0], into)
    token_grad = grad_middle + grad_norm
    ffout_sum.finish(*self_sum.sent, cost=lasting(100))
    ffin_sum.rows(ffout_sum.total)
    output_state = matmuls(
        [product],
        [(ffout, 0)],
        NN,
        "output_state",
        [ffout_sum.total, ffin_sum.near],
        [later, jnp.broadcast_to(live, tokens.shape[:2] + (1,))],
    ).reshape(tokens.shape)
    self_sum.step("z", output_state)
    self_sum.send()
    cross_sum.finish(*self_sum.sent, cost=lasting(100))
    grad_table = jnp.einsum(
        "nb,hn->bh", hot, diagonals.reshape(heads, seq_len), precision=lax.Precision.HIGHEST
    )
    small = jnp.stack([gain_self, gain_cross, gain_feed]).reshape(3, fsdp, shard)
    small = jnp.concatenate(
        [
            jnp.transpose(small, (1, 0, 2)).reshape(fsdp, 3 * shard),
            grad_table.reshape(fsdp, table_rows * heads),
        ],
        axis=1,
    )
    small = held_back(jnp.pad(small, ((0, 0), (0, -small_count % 128))), self_sum.sent)
    small = sum_owners(place, sum_replicas(place, small))
    ffout_sum.rows(cross_sum.total)
    cross_sum.rows(ffout_sum.near)
    self_sum.finish(cross_sum.near)
    self_sum.rows()

    def matrices(stage, size):
        near, far = stage.done()
        return [
            jnp.concatenate([near[:, i : i + size], far[:, i : i + size]], axis=1)
            for i in range(0, near.shape[1], size)
        ]

    cross_grads = matrices(cross_sum, part)
    self_grads = matrices(self_sum, part)
    qkv_grad = jnp.stack([jnp.stack(self_grads), jnp.stack(cross_grads[:3])])[None]
    out_grad = jnp.stack([cross_grads[4], cross_grads[3]])[None]
    ffin_grad = jnp.stack(matrices(ffin_sum, half))[None]
    ffout_grad = matrices(ffout_sum, part)[0][None]
    return (
        output_state,
        token_grad,
        encoder_grad,
        qkv_grad,
        out_grad,
        ffin_grad,
        ffout_grad,
        small[: 3 * shard].reshape(1, 3, shard),
        small[3 * shard : small_count].reshape(table_rows, heads),
    )


def solution(mesh):
    in_specs = (
        P(("rep", "fsdp"), None, None),
        P(("rep", "fsdp"), None, None),
        P(("rep", "fsdp"), None, None),
        P(None, None, None, "fsdp", None),
        P(None, None, "fsdp", None),
        P(None, None, "fsdp", None),
        P(None, "fsdp", None),
        P(None, None, "fsdp"),
        P("fsdp", None),
        P(("rep", "fsdp")),
        P(("rep", "fsdp")),
    )
    out_specs = (
        P(("rep", "fsdp"), None, None),
        P(("rep", "fsdp"), None, None),
        P(("rep", "fsdp"), None, None),
        P(None, None, None, "fsdp", None),
        P(None, None, "fsdp", None),
        P(None, None, "fsdp", None),
        P(None, "fsdp", None),
        P(None, None, "fsdp"),
        P("fsdp", None),
    )
    return jax.shard_map(
        functools.partial(per_device, mesh.shape["rep"], mesh.shape["fsdp"]),
        mesh=mesh, in_specs=in_specs, out_specs=out_specs, check_vma=False
    )
```

```python
import functools

import jax
import jax.numpy as jnp
from jax import lax
from jax.experimental import pallas as pl
from jax.experimental.pallas import tpu as pltpu
from jax.sharding import PartitionSpec as P

EPS = 1e-06
STEPS = (19, 21, 24, 27, 31, 35, 40, 46, 52, 59, 67, 77, 87, 99, 113)


Z = 4


class Place:
    def __init__(self, rep, fsdp):
        self.rep, self.fsdp = rep, fsdp
        self.nx = fsdp // Z
        r = lax.axis_index("rep")
        f = lax.axis_index("fsdp")
        self.c, self.y = r % 2, (r // 2) % 2
        self.z, self.x = f // self.nx, f % self.nx
        self.q = 2 * self.y + self.c

    def core(self, v):
        return lax.ppermute(v, "rep", [(i, i ^ 1) for i in range(self.rep)])

    def across(self, v, bit):
        return lax.ppermute(v, "rep", [(i, i ^ bit) for i in range(self.rep)])

    def along_x(self, v, d):
        nx = self.nx
        return lax.ppermute(
            v, "fsdp", [(i, i // nx * nx + (i % nx + d) % nx) for i in range(self.fsdp)]
        )

    def along_z(self, v, d):
        return lax.ppermute(
            v, "fsdp", [(i, (i + d * self.nx) % self.fsdp) for i in range(self.fsdp)]
        )


def low(v):
    return v.astype(jnp.bfloat16)


def wide(v):
    return v.astype(jnp.float32)


def pick(v, i, axis=0):
    return lax.dynamic_index_in_dim(v, i, axis, keepdims=False)


FREE = pl.CostEstimate(flops=0, bytes_accessed=0, transcendentals=0)


def lasting(microseconds):
    return pl.CostEstimate(
        flops=int(microseconds * 1e9), bytes_accessed=0, transcendentals=0
    )


VMEM = pl.BlockSpec(memory_space=pltpu.VMEM)
SMEM = pl.BlockSpec(memory_space=pltpu.SMEM)


def shape_of(shape, dtype=jnp.bfloat16):
    return jax.ShapeDtypeStruct(shape, dtype)


def call(body, ins, outs, name, waits=(), specs=None, vmem=16, cost=FREE, **kw):
    waits = list(waits)
    count, late = len(ins), len(ins) + len(waits)

    def kernel(*refs):
        body(*refs[:count], *refs[late:])

    return pl.pallas_call(
        kernel,
        in_specs=list(specs or [VMEM] * count) + [pl.BlockSpec(memory_space=pl.ANY)] * len(waits),
        out_shape=outs,
        name=name,
        compiler_params=pltpu.CompilerParams(vmem_limit_bytes=vmem * 1024 * 1024),
        cost_estimate=cost,
        **kw,
    )(*ins, *waits)


def stack_kernel(*refs):
    for k, ref in enumerate(refs[:-1]):
        refs[-1][k] = ref[...]


def copy_kernel(ref, out):
    out[...] = ref[...]


def stacked(values, waits=()):
    shape = shape_of((len(values),) + values[0].shape, values[0].dtype)
    return call(stack_kernel, values, shape, "stack", waits)


def held_back(value, waits):
    return call(copy_kernel, [value], shape_of(value.shape, value.dtype), "hold", waits)


LANES = 128
SMALL_ROWS = 16


def assemble_kernel(where_ref, *refs, parts, nx, sizes, small):
    outs = refs[len(parts) :]
    c, y, z, x = (where_ref[i] for i in range(4))
    for ref, (dc, dy, dx) in zip(refs, parts):
        core = c ^ dc
        row = y ^ dy
        col = lax.rem(x - dx + nx, nx)
        for k in range(Z):
            f = lax.rem(z - k + Z, Z) * nx + col
            at = 0
            for out, (m, h, w) in zip(outs, sizes):
                for t in range(w // LANES):
                    lane = pl.ds(pl.multiple_of(core * w + t * LANES, LANES), LANES)
                    for i in range(m):
                        out[i, f, row, :, lane] = ref[k, at : at + h, :]
                        at += h
            if small and (dc, dy) == (0, 0):
                outs[-1][f] = ref[k, at : at + SMALL_ROWS, :]


class Gather:
    def __init__(self, place, shards, y_last, small=None):
        self.place, self.y_last, self.small = place, y_last, small
        self.sizes, rows = [], []
        for shard in shards:
            m, h, w = shard.shape[0], shard.shape[1] // 2, shard.shape[2] // 2
            self.sizes.append((m, h, w))
            cut = lax.dynamic_slice(shard, (0, place.y * h, place.c * w), (m, h, w))
            cut = jnp.transpose(cut.reshape(m, h, w // LANES, LANES), (2, 0, 1, 3))
            rows.append(cut.reshape(-1, LANES))
        if small is not None:
            rows.append(small)
        self.piece = rows[0] if len(rows) == 1 else jnp.concatenate(rows)

    def first(self):
        self.pieces = [self.piece] + [self.place.along_z(self.piece, d) for d in range(1, Z)]

    def second(self, *waits):
        self.stack = stacked(self.pieces, waits)

    def send(self):
        place, stack = self.place, self.stack
        self.held = {(0, 0): stack}
        for d in range(1, place.nx):
            self.held[0, d] = place.along_x(stack, d)
        self.held[1, 0] = place.across(stack, 2)

    def turn(self, *waits):
        self.onward = []
        for d in range(1, self.place.nx) if self.y_last else (0,):
            key = (0, d) if self.y_last else (1, 0)
            if waits:
                self.held[key] = held_back(self.held[key], waits)
            self.onward.append(self.held[key])

    def third(self):
        place, nx = self.place, self.place.nx
        for d in range(1, nx):
            if self.y_last:
                self.held[1, d] = place.across(self.held[0, d], 2)
            else:
                self.held[1, d] = place.along_x(self.held[1, 0], d)

    def settle(self, *waits):
        for d in range(1, self.place.nx):
            self.held[1, d] = held_back(self.held[1, d], waits)

    def whole(self, *waits):
        place = self.place
        parts, arrays = [], []
        for key, value in self.held.items():
            parts += [(0,) + key, (1,) + key]
            arrays += [value, place.across(value, 1)]
        shapes = [shape_of((m, place.fsdp, 2, h, 2 * w)) for m, h, w in self.sizes]
        if self.small is not None:
            shapes.append(shape_of((place.fsdp, SMALL_ROWS, LANES)))
        where = jnp.stack([place.c, place.y, place.z, place.x]).astype(jnp.int32)
        body = functools.partial(
            assemble_kernel,
            parts=tuple(parts),
            nx=place.nx,
            sizes=tuple(self.sizes),
            small=self.small is not None,
        )
        specs = [SMEM] + [VMEM] * len(arrays)
        full = call(body, [where] + arrays, shapes, "assemble", waits, specs, vmem=28)
        whole = [
            v.reshape(m, place.fsdp * 2 * h, 2 * w) for v, (m, h, w) in zip(full, self.sizes)
        ]
        return whole + list(full[len(whole) :])


def step_kernel(where_ref, kept_ref, *refs, axis, count, lead):
    got, keep_ref, send_refs = refs[: -count], refs[-count], refs[len(refs) - count + 1 :]
    own = where_ref[0]
    rest = [()]
    for size in lead[:axis] + lead[axis + 1 :]:
        rest = [r + (i,) for r in rest for i in range(size)]

    def value(at):
        total = kept_ref[at]
        for ref in got:
            total = total + ref[at].astype(jnp.float32)
        return total

    for r in rest:
        keep_ref[r] = value(r[:axis] + (own,) + r[axis:])
        for d, ref in enumerate(send_refs, 1):
            there = lax.rem(own + d, count)
            ref[r] = value(r[:axis] + (there,) + r[axis:]).astype(jnp.bfloat16)


def total_kernel(kept_ref, *refs):
    total = kept_ref[...]
    for ref in refs[:-1]:
        total = total + ref[...].astype(jnp.float32)
    refs[-1][...] = total


def rows_kernel(where_ref, total_ref, other_ref, out):
    h = total_ref.shape[0]
    y = where_ref[0]
    out[pl.ds(pl.multiple_of(y * h, 8), h), :] = total_ref[...]
    out[pl.ds(pl.multiple_of((1 - y) * h, 8), h), :] = other_ref[...]


class Reduce:
    def __init__(self, place, sent, kept):
        self.place = place
        lead = (Z, place.nx, 2)
        self.sent = [sent]
        self.kept = kept.reshape(lead + kept.shape[2:])
        self.axes = ["z", "x", "y"]
        self.name = "core"

    def send(self):
        place = self.place
        if self.name == "core":
            self.got = [place.across(self.sent[0], 1).reshape(self.kept.shape)]
        elif self.name == "y":
            self.got = [place.across(self.sent[0], 2)]
        else:
            move = place.along_x if self.name == "x" else place.along_z
            self.got = [move(v, d) for d, v in enumerate(self.sent, 1)]

    def step(self, name, *waits, cost=FREE):
        place = self.place
        axis = self.axes.index(name)
        lead, tail = self.kept.shape[:-2], self.kept.shape[-2:]
        count = lead[axis]
        left = lead[:axis] + lead[axis + 1 :] + tail
        own = {"z": place.z, "x": place.x, "y": place.y}[name].reshape(1).astype(jnp.int32)
        outs = [shape_of(left, jnp.float32)] + [shape_of(left)] * (count - 1)
        body = functools.partial(step_kernel, axis=axis, count=count, lead=lead)
        ins = [own, self.kept] + self.got
        specs = [SMEM] + [VMEM] * (len(ins) - 1)
        self.kept, *self.sent = call(
            body, ins, outs, "step_" + name, waits, specs, vmem=20, cost=cost
        )
        self.axes.remove(name)
        self.name = name

    def finish(self, *waits, cost=FREE):
        place = self.place
        shape = shape_of(self.kept.shape, jnp.float32)
        total = call(total_kernel, [self.kept] + self.got, shape, "total", waits, cost=cost)
        bit = 4
        while bit < place.rep:
            total = total + place.across(total, bit)
            bit *= 2
        self.total, self.other = total, place.across(total, 2)

    def rows(self, *waits, cost=FREE):
        place = self.place
        h, w = self.total.shape
        ins = [place.y.reshape(1).astype(jnp.int32), self.total, self.other]
        out = shape_of((2 * h, w), jnp.float32)
        self.near = call(rows_kernel, ins, out, "rows", waits, [SMEM, VMEM, VMEM], cost=cost)
        self.far = place.across(self.near, 1)

    def done(self):
        first = self.place.c == 0
        return jnp.where(first, self.near, self.far), jnp.where(first, self.far, self.near)


def sum_replicas(place, partial):
    bit = 1
    while bit < place.rep:
        partial = partial + place.across(partial, bit)
        bit *= 2
    return partial


def sum_owners(place, partial):
    total = partial.reshape(Z, place.nx, -1)
    near = pick(total, place.x, 1)
    for d in range(1, place.nx):
        near = near + place.along_x(pick(total, (place.x + d) % place.nx, 1), d)
    mine = pick(near, place.z)
    for d in range(1, Z):
        mine = mine + place.along_z(pick(near, (place.z + d) % Z), d)
    return mine


NEGATIVE = -1e30
TILE = 256
PAIR = 128


def dot(a, b, dims):
    return lax.dot_general(a, b, (dims, ((), ())), preferred_element_type=jnp.float32)


NT = ((1,), (1,))
NN = ((1,), (0,))
TN = ((0,), (0,))


def turned(v):
    return v.astype(jnp.float32).T


def half_mask(j):
    return lax.broadcasted_iota(jnp.int32, (1, PAIR), 1) // (PAIR // 2) == j


def masked_scores(k, qm, toe, length, t, causal):
    scores = dot(k, qm, NT)
    rows = scores.shape[0]
    key = lax.broadcasted_iota(jnp.int32, (rows, TILE), 0)
    if causal:
        bias = toe[:, :TILE]
        if t:
            bias = jnp.concatenate([toe[:, TILE:], bias], axis=0)
        scores = scores + bias
        query = lax.broadcasted_iota(jnp.int32, (rows, TILE), 1) + t * TILE
        allowed = key <= jnp.minimum(query, length - 1)
    else:
        allowed = key < length
    return jnp.where(allowed, scores, NEGATIVE)


def spread(row_ref, toe_ref):
    for j in range(2):
        row = jnp.broadcast_to(row_ref[0, j : j + 1, :], (TILE, 2 * TILE))
        toe_ref[j] = pltpu.roll(row, 0, 1, stride=1, stride_axis=0)


def forward_kernel(causal, len_ref, *refs):
    if causal:
        q_ref, k_ref, v_ref, row_ref, o_ref, lse_ref, toe_ref = refs
    else:
        q_ref, k_ref, v_ref, o_ref, lse_ref = refs
        toe_ref = None
    s = pl.program_id(1)
    length = len_ref[s]
    if causal:

        @pl.when(s == 0)
        def _():
            spread(row_ref, toe_ref)

    q, k, v = q_ref[0], k_ref[0], v_ref[0]
    v_turned = turned(v).astype(jnp.bfloat16)
    cells = [(t, j) for t in range(q.shape[0] // TILE) for j in range(2)]

    def score(t, j):
        seen = (t + 1) * TILE if causal else k.shape[0]
        qm = jnp.where(half_mask(j), q[t * TILE : (t + 1) * TILE], 0)
        return masked_scores(k[:seen], qm, toe_ref[j] if causal else None, length, t, causal)

    outs = []
    ahead = score(*cells[0])
    for i, (t, j) in enumerate(cells):
        scores = ahead
        if i + 1 < len(cells):
            ahead = score(*cells[i + 1])
        here = slice(t * TILE, (t + 1) * TILE)
        top = jnp.max(scores, axis=0, keepdims=True)
        grown = jnp.exp(scores - top)
        total = jnp.sum(grown, axis=0, keepdims=True)
        lse_ref[0, 0, j : j + 1, here] = top + jnp.log(total)
        chances = (grown * (1.0 / total)).astype(jnp.bfloat16)
        outs.append(dot(v_turned[j * 64 : (j + 1) * 64, : scores.shape[0]], chances, NN))
        if j:
            o_ref[0, here, :] = turned(jnp.concatenate(outs, axis=0)).astype(jnp.bfloat16)
            outs = []


def diagonal_sums(v):
    width = v.shape[1]
    groups = v[:8]
    for a in range(8, v.shape[0], 8):
        groups = groups + pltpu.roll(v[a : a + 8], width - a, 1)
    total = groups[:1]
    for b in range(1, 8):
        total = total + pltpu.roll(groups[b : b + 1], width - b, 1)
    return total


def backward_kernel(causal, len_ref, *refs):
    if causal:
        q_ref, k_ref, v_ref, do_ref, lse_ref, row_ref = refs[:6]
        dq_ref, dk_ref, dv_ref, diag_ref, toe_ref, sum_ref = refs[6:]
    else:
        q_ref, k_ref, v_ref, do_ref, lse_ref = refs[:5]
        dq_ref, dk_ref, dv_ref = refs[5:]
        toe_ref = None
    s = pl.program_id(1)
    length = len_ref[s]
    if causal:

        @pl.when(s == 0)
        def _():
            spread(row_ref, toe_ref)
            sum_ref[...] = jnp.zeros_like(sum_ref)

    q, k, v, do = q_ref[0], k_ref[0], v_ref[0], do_ref[0]
    k_turned = turned(k).astype(jnp.bfloat16)
    tiles = q.shape[0] // TILE
    dk = [None] * tiles
    dv = [None] * tiles
    cells = [(t, j) for t in range(tiles) for j in range(2)]
    outs = []

    def add(held, value):
        return value if held is None else held + value

    def score(t, j):
        seen = (t + 1) * TILE if causal else k.shape[0]
        here = slice(t * TILE, (t + 1) * TILE)
        qm = jnp.where(half_mask(j), q[here], 0)
        dom = jnp.where(half_mask(j), do[here], 0)
        scores = masked_scores(k[:seen], qm, toe_ref[j] if causal else None, length, t, causal)
        return scores, dot(v[:seen], dom, NT), qm, dom

    def finish(t, j, chances, d_scores, qm, dom):
        seen = d_scores.shape[0]
        outs.append(dot(k_turned[j * 64 : (j + 1) * 64, :seen], d_scores, NN))
        dv_part = dot(chances, dom, NN)
        dk_part = dot(d_scores, qm, NN)
        for b in range(seen // TILE):
            rows = slice(b * TILE, (b + 1) * TILE)
            dv[b] = add(dv[b], dv_part[rows])
            dk[b] = add(dk[b], dk_part[rows])
        if causal:
            if t:
                sum_ref[j, :, TILE:] += d_scores[: t * TILE].astype(jnp.float32)
            sum_ref[j, :, :TILE] += d_scores[t * TILE :].astype(jnp.float32)
        if j:
            here = slice(t * TILE, (t + 1) * TILE)
            dq_ref[0, here, :] = turned(jnp.concatenate(outs, axis=0)).astype(jnp.bfloat16)
            outs.clear()

    ahead = score(*cells[0])
    behind = None
    for i, (t, j) in enumerate(cells):
        scores, d_chances, qm, dom = ahead
        if i + 1 < len(cells):
            ahead = score(*cells[i + 1])
        here = slice(t * TILE, (t + 1) * TILE)
        chances = jnp.exp(scores - lse_ref[0, 0, j : j + 1, here])
        delta = jnp.sum(chances * d_chances, axis=0, keepdims=True)
        d_scores = (chances * (d_chances - delta)).astype(jnp.bfloat16)
        if behind is not None:
            finish(*behind)
        behind = (t, j, chances.astype(jnp.bfloat16), d_scores, qm, dom)
    finish(*behind)
    for b in range(tiles):
        rows = slice(b * TILE, (b + 1) * TILE)
        dk_ref[0, rows, :] = dk[b].astype(jnp.bfloat16)
        dv_ref[0, rows, :] = dv[b].astype(jnp.bfloat16)
    if causal:

        @pl.when(s == pl.num_programs(1) - 1)
        def _():
            for j in range(2):
                diag_ref[0, j : j + 1, :] = diagonal_sums(sum_ref[j])


def attend(kind, q, k, v, lengths, row=None, do=None, lse=None, waits=()):
    count, slots, width = q.shape
    pairs = width // PAIR
    assert slots == 2 * TILE and k.shape[1] == 2 * TILE
    block = pl.BlockSpec((1, slots, PAIR), lambda p, s: (s, 0, p))
    lse_block = pl.BlockSpec((1, 1, 2, slots), lambda p, s: (s, p, 0, 0))
    row_block = pl.BlockSpec((1, 2, slots), lambda p, s: (p, 0, 0))
    state = jax.ShapeDtypeStruct(q.shape, jnp.bfloat16)
    causal = row is not None
    ins, specs = [lengths, q, k, v], [pl.BlockSpec(memory_space=pltpu.SMEM), block, block, block]
    if kind == "forward":
        body = forward_kernel
        outs = [state, jax.ShapeDtypeStruct((count, pairs, 2, slots), jnp.float32)]
        out_specs = [block, lse_block]
    else:
        body = backward_kernel
        ins += [do, lse]
        specs += [block, lse_block]
        outs = [state] * 3
        out_specs = [block] * 3
    scratch = []
    if causal:
        ins.append(row)
        specs.append(row_block)
        scratch.append(pltpu.VMEM((2, TILE, 2 * TILE), jnp.float32))
        if kind == "backward":
            outs.append(jax.ShapeDtypeStruct(row.shape, jnp.float32))
            out_specs.append(row_block)
            scratch.append(pltpu.VMEM((2, TILE, 2 * TILE), jnp.float32))
    return call(
        functools.partial(body, causal),
        ins,
        outs,
        ("self_" if causal else "cross_") + kind,
        waits,
        specs,
        vmem=16,
        cost=lasting(200),
        grid=(pairs, count),
        out_specs=out_specs,
        scratch_shapes=scratch,
    )


FF_TILE = 256
ROW_TILE = 256


def feed_kernel(n_ref, df_ref, in_ref, out_ref, product_ref, gate_ref, up_ref):
    scale, cubic = 0.7978845608028654, 0.044715

    def dots(r):
        rows = slice(r * ROW_TILE, (r + 1) * ROW_TILE)
        n = n_ref[rows, :]
        return (
            dot(n, in_ref[0], NN),
            dot(n, in_ref[1], NN),
            dot(df_ref[rows, :], out_ref[...], NT),
        )

    count = n_ref.shape[0] // ROW_TILE
    ahead = dots(0)
    for r in range(count):
        gate, up, d_product = ahead
        if r + 1 < count:
            ahead = dots(r + 1)
        rows = slice(r * ROW_TILE, (r + 1) * ROW_TILE)
        square = gate * gate
        bend = jnp.tanh(scale * (gate + cubic * (square * gate)))
        half = 0.5 * (1.0 + bend)
        gelu = gate * half
        slope = half + (0.5 * scale) * gate * (1.0 - bend * bend) * (1.0 + 3 * cubic * square)
        product_ref[rows, :] = (gelu * up).astype(jnp.bfloat16)
        gate_ref[rows, :] = (d_product * up * slope).astype(jnp.bfloat16)
        up_ref[rows, :] = (d_product * gelu).astype(jnp.bfloat16)


def feed(n, df, ffin, ffout):
    count, width = n.shape
    hidden = ffout.shape[0]
    whole = pl.BlockSpec((count, width), lambda i: (0, 0))
    tile = pl.BlockSpec((count, FF_TILE), lambda i: (0, i))
    state = jax.ShapeDtypeStruct((count, hidden), jnp.bfloat16)
    specs = [
        whole,
        whole,
        pl.BlockSpec((2, width, FF_TILE), lambda i: (0, 0, i)),
        pl.BlockSpec((FF_TILE, width), lambda i: (i, 0)),
    ]
    return call(
        feed_kernel,
        [n, df, ffin, ffout],
        [state] * 3,
        "feed",
        (),
        specs,
        cost=lasting(100),
        vmem=24,
        grid=(hidden // FF_TILE,),
        out_specs=[tile] * 3,
    )


def matmuls_kernel(*refs, count, dims, ends):
    total = dot(refs[0][...], refs[count][0], dims)
    for i in range(1, count):
        total = total + dot(refs[i][...], refs[count + i][0], dims)
    if ends:
        total = (total + refs[2 * count][...]) * refs[2 * count + 1][...]
    refs[-1][...] = total.astype(refs[-1].dtype)


def matmuls(lefts, weights, dims, name, waits=(), ends=(), cost=FREE, dtype=jnp.float32):
    lefts = [v.reshape(-1, v.shape[-1]) for v in lefts]
    ends = [v.reshape(-1, v.shape[-1]) for v in ends]
    rows = lefts[0].shape[0]
    width = weights[0][0].shape[1 if dims == NT else 2]

    def tile(v):
        return pl.BlockSpec((ROW_TILE, v.shape[1]), lambda i: (i, 0))

    def layer(v, k):
        return pl.BlockSpec((1,) + v.shape[1:], lambda i: (k, 0, 0))

    out = shape_of((rows, width), dtype)
    return call(
        functools.partial(matmuls_kernel, count=len(lefts), dims=dims, ends=bool(ends)),
        lefts + [w for w, _ in weights] + ends,
        out,
        name,
        waits,
        [tile(v) for v in lefts] + [layer(*w) for w in weights] + [tile(v) for v in ends],
        vmem=24,
        cost=cost,
        grid=(rows // ROW_TILE,),
        out_specs=tile(out),
    )


def grads_kernel(where_ref, *refs, pairs, lefts, rights):
    left_refs, right_refs = refs[:lefts], refs[lefts : lefts + rights]
    sent_ref, kept_ref = refs[-2:]
    first = where_ref[0] == 0
    for i, left in enumerate(left_refs):
        for m in range(0, left.shape[1], ROW_TILE):
            rows = slice(m, m + ROW_TILE)
            block = turned(left[:, rows]).astype(jnp.bfloat16)
            at = 0
            for k, j in pairs:
                right = right_refs[j]
                w = right.shape[1] // 2
                if k == i:
                    both = dot(block, right[...], NN)
                    near, far = both[:, :w], both[:, w:]
                    sent_ref[rows, at : at + w] = jnp.where(first, far, near).astype(jnp.bfloat16)
                    kept_ref[rows, at : at + w] = jnp.where(first, near, far)
                at += w


def stage_grads(place, lefts, rights, pairs, *waits, cost=FREE):
    lefts = [v.reshape(-1, v.shape[-1]) for v in lefts]
    rights = [v.reshape(-1, v.shape[-1]) for v in rights]
    height = lefts[0].shape[1]
    width = sum(rights[j].shape[1] // 2 for _, j in pairs)
    ins = [place.c.reshape(1).astype(jnp.int32)] + lefts + rights
    sent, kept = call(
        functools.partial(
            grads_kernel, pairs=tuple(pairs), lefts=len(lefts), rights=len(rights)
        ),
        ins,
        [shape_of((height, width)), shape_of((height, width), jnp.float32)],
        "grads",
        waits,
        [SMEM] + [VMEM] * (len(ins) - 1),
        vmem=28,
        cost=cost,
    )
    shape = (place.fsdp, 2, height // place.fsdp // 2, width)
    return Reduce(place, sent.reshape(shape), kept.reshape(shape))


def rms_scale(values, factor):
    return values * lax.rsqrt(jnp.mean(values * values, axis=-1, keepdims=True) + EPS) * factor


def rms_back(values, factor, grad_out):
    return jax.vjp(rms_scale, values, factor)[1](grad_out)


def project(a, w):
    return jnp.einsum("vgq,qy->vgy", a, w, preferred_element_type=jnp.float32)


def project_back(a, w):
    return jnp.einsum("gjr,fr->gjf", a, w, preferred_element_type=jnp.float32)


def bucket_hot(extent, buckets):
    distance = jnp.arange(extent, dtype=jnp.int32)
    far = 16 + sum(((distance >= border).astype(jnp.int32) for border in STEPS))
    bucket = jnp.where(distance < 16, distance, far)
    return (bucket[:, None] == jnp.arange(buckets, dtype=jnp.int32)).astype(jnp.float32)


def per_device(
    rep,
    fsdp,
    tokens,
    encoder_states,
    cotangent,
    qkv_weight,
    out_weight,
    ffin_weight,
    ffout_weight,
    norm_gains,
    bias_table,
    lengths,
    enc_lengths,
):
    place = Place(rep, fsdp)
    seq_len, width = tokens.shape[1:]
    table_rows, heads = bias_table.shape
    shard = qkv_weight.shape[3]
    first = place.c == 0
    half = ffin_weight.shape[3] // 2
    part = width // 2

    small_count = 3 * shard + table_rows * heads
    small = jnp.concatenate([norm_gains.reshape(-1), bias_table.reshape(-1)])
    small = jnp.pad(small, (0, SMALL_ROWS * LANES - small_count)).reshape(SMALL_ROWS, LANES)
    stages = [
        Gather(place, [jnp.concatenate([qkv_weight[0, 0], out_weight[0, :1]])], True, small),
        Gather(place, [jnp.concatenate([qkv_weight[0, 1], out_weight[0, 1:]])], False),
        Gather(place, [ffin_weight[0], ffout_weight], True),
    ]
    for stage in stages:
        stage.first()
    stages[0].second()
    stages[0].send()
    stages[1].second()
    stages[0].turn(stages[1].stack, stages[0].held[1, 0])
    stages[0].third()
    stages[2].second()
    self_w, small = stages[0].whole(stages[2].stack)
    small = small.reshape(fsdp, SMALL_ROWS * LANES)
    gains = small[:, : 3 * shard].reshape(fsdp, 3, shard)
    gains = wide(jnp.transpose(gains, (1, 0, 2)).reshape(3, width))
    table = wide(small[:, 3 * shard : small_count].reshape(fsdp * table_rows, heads))
    hot = bucket_hot(seq_len, fsdp * table_rows)
    row = jnp.einsum("nb,bh->hn", hot, table, precision=lax.Precision.HIGHEST)
    row = row.reshape(heads // 2, 2, seq_len)

    live = wide(jnp.arange(seq_len, dtype=jnp.int32)[None, :] < lengths[:, None])[:, :, None]
    stream = wide(tokens)
    normed_self = low(rms_scale(stream, gains[0]))
    q1, k1, v1 = (low(project(normed_self, self_w[i])) for i in range(3))
    stages[1].send()
    stages[1].turn(self_w)
    stages[1].third()
    stages[2].send()
    ready = stages[1].onward + [stages[2].stack]
    o1, lse1 = attend("forward", q1, k1, v1, lengths, row, waits=ready)
    middle = stream + project(o1, self_w[3])
    normed_cross = low(rms_scale(middle, gains[1]))
    cross_w, = stages[1].whole(o1)
    q2 = low(project(normed_cross, cross_w[0]))
    k2, v2 = (low(project(encoder_states, cross_w[i])) for i in (1, 2))
    stages[2].turn(cross_w)
    stages[2].third()
    o2, lse2 = attend("forward", q2, k2, v2, enc_lengths, waits=stages[2].onward)
    later = middle + project(o2, cross_w[3])
    normed_feed = low(rms_scale(later, gains[2]))
    stages[2].settle(o2)
    ffin, ffout = stages[2].whole(o2)

    def flat(v):
        return v.reshape(-1, v.shape[-1])

    grad = wide(cotangent) * live
    grad_low = low(grad)
    product, grad_gate, grad_upward = (
        v.reshape(tokens.shape[:2] + (2 * half,))
        for v in feed(flat(normed_feed), flat(grad_low), ffin, ffout[0])
    )

    ffin_sum = stage_grads(place, [normed_feed], [grad_gate, grad_upward], [(0, 0), (0, 1)])
    ffin_sum.send()
    ffout_sum = stage_grads(place, [product], [grad_low], [(0, 0)], *ffin_sum.sent)
    ffin_sum.step("x", *ffout_sum.sent)
    ffout_sum.send()
    grad_normed = matmuls(
        [grad_gate, grad_upward], [(ffin, 0), (ffin, 1)], NT, "grad_normed", ffin_sum.sent, cost=lasting(100)
    ).reshape(tokens.shape)
    grad_norm, gain_feed = rms_back(later, gains[2], grad_normed)
    grad_later = grad + grad_norm
    ffout_sum.step("y", *ffin_sum.sent)

    da2 = low(grad_later)
    do = low(project_back(da2, cross_w[3]))
    ready = ffout_sum.sent + ffin_sum.sent
    ffin_sum.send()
    ffout_sum.send()
    dq2, dk2, dv2 = attend("backward", q2, k2, v2, enc_lengths, None, do, lse2, ready)
    ffin_sum.step("y", dq2)
    ffout_sum.step("x", *ffin_sum.sent)
    ffin_sum.send()
    ffout_sum.send()
    grad_norm, gain_cross = rms_back(middle, gains[1], project_back(dq2, cross_w[0]))
    grad_middle = grad_later + grad_norm
    da1 = low(grad_middle)
    cross_sum = stage_grads(
        place,
        [normed_cross, encoder_states, o2, o1],
        [dq2, dk2, dv2, da2, da1],
        [(0, 0), (1, 1), (1, 2), (2, 3), (3, 4)],
        *ffout_sum.sent,
        cost=lasting(100),
    )
    cross_sum.send()
    ffin_sum.step("z", *cross_sum.sent)
    do = matmuls(
        [da1],
        [(self_w, 3)],
        NT,
        "self_do",
        ffin_sum.sent,
        cost=lasting(100),
        dtype=jnp.bfloat16,
    ).reshape(tokens.shape)
    cross_sum.step("y", do)

    ready = cross_sum.sent + ffin_sum.sent
    cross_sum.send()
    ffin_sum.send()
    dq1, dk1, dv1, diagonals = attend("backward", q1, k1, v1, lengths, row, do, lse1, ready)
    cross_sum.step("x", dq1)
    cross_sum.send()
    self_sum = stage_grads(
        place, [normed_self], [dq1, dk1, dv1], [(0, 0), (0, 1), (0, 2)], *cross_sum.sent
    )
    self_sum.send()
    ffout_sum.step("z", *self_sum.sent, cost=lasting(100))
    ffin_sum.finish(*ffout_sum.sent)
    ffout_sum.send()
    self_sum.step("y", *ffout_sum.sent)
    self_sum.send()
    encoder_grad = matmuls(
        [dk2, dv2],
        [(cross_w, 1), (cross_w, 2)],
        NT,
        "encoder_grad",
        self_sum.sent,
        cost=lasting(100),
    ).reshape(tokens.shape)
    into = matmuls(
        [dq1, dk1, dv1],
        [(self_w, 0), (self_w, 1), (self_w, 2)],
        NT,
        "into",
        [encoder_grad, ffin_sum.total],
    ).reshape(tokens.shape)
    cross_sum.step("z", into)
    cross_sum.send()
    self_sum.step("x", *cross_sum.sent)
    self_sum.send()
    grad_norm, gain_self = rms_back(stream, gains[0], into)
    token_grad = grad_middle + grad_norm
    ffout_sum.finish(*self_sum.sent, cost=lasting(100))
    ffin_sum.rows(ffout_sum.total)
    output_state = matmuls(
        [product],
        [(ffout, 0)],
        NN,
        "output_state",
        [ffout_sum.total, ffin_sum.near],
        [later, jnp.broadcast_to(live, tokens.shape[:2] + (1,))],
    ).reshape(tokens.shape)
    self_sum.step("z", output_state)
    self_sum.send()
    cross_sum.finish(*self_sum.sent, cost=lasting(100))
    diagonals = held_back(diagonals, [output_state])
    grad_table = jnp.einsum(
        "nb,hn->bh", hot, diagonals.reshape(heads, seq_len), precision=lax.Precision.HIGHEST
    )
    small = jnp.stack([gain_self, gain_cross, gain_feed]).reshape(3, fsdp, shard)
    small = jnp.concatenate(
        [
            jnp.transpose(small, (1, 0, 2)).reshape(fsdp, 3 * shard),
            grad_table.reshape(fsdp, table_rows * heads),
        ],
        axis=1,
    )
    small = held_back(jnp.pad(small, ((0, 0), (0, -small_count % 128))), self_sum.sent)
    small = sum_owners(place, sum_replicas(place, small))
    ffout_sum.rows(cross_sum.total)
    cross_sum.rows(ffout_sum.near)
    self_sum.finish(cross_sum.near)
    self_sum.rows()

    def matrices(stage, size):
        near, far = stage.done()
        return [
            jnp.concatenate([near[:, i : i + size], far[:, i : i + size]], axis=1)
            for i in range(0, near.shape[1], size)
        ]

    cross_grads = matrices(cross_sum, part)
    self_grads = matrices(self_sum, part)
    qkv_grad = jnp.stack([jnp.stack(self_grads), jnp.stack(cross_grads[:3])])[None]
    out_grad = jnp.stack([cross_grads[4], cross_grads[3]])[None]
    ffin_grad = jnp.stack(matrices(ffin_sum, half))[None]
    ffout_grad = matrices(ffout_sum, part)[0][None]
    return (
        output_state,
        token_grad,
        encoder_grad,
        qkv_grad,
        out_grad,
        ffin_grad,
        ffout_grad,
        small[: 3 * shard].reshape(1, 3, shard),
        small[3 * shard : small_count].reshape(table_rows, heads),
    )


def solution(mesh):
    in_specs = (
        P(("rep", "fsdp"), None, None),
        P(("rep", "fsdp"), None, None),
        P(("rep", "fsdp"), None, None),
        P(None, None, None, "fsdp", None),
        P(None, None, "fsdp", None),
        P(None, None, "fsdp", None),
        P(None, "fsdp", None),
        P(None, None, "fsdp"),
        P("fsdp", None),
        P(("rep", "fsdp")),
        P(("rep", "fsdp")),
    )
    out_specs = (
        P(("rep", "fsdp"), None, None),
        P(("rep", "fsdp"), None, None),
        P(("rep", "fsdp"), None, None),
        P(None, None, None, "fsdp", None),
        P(None, None, "fsdp", None),
        P(None, None, "fsdp", None),
        P(None, "fsdp", None),
        P(None, None, "fsdp"),
        P("fsdp", None),
    )
    return jax.shard_map(
        functools.partial(per_device, mesh.shape["rep"], mesh.shape["fsdp"]),
        mesh=mesh, in_specs=in_specs, out_specs=out_specs, check_vma=False
    )
```

```python
import functools

import jax
import jax.numpy as jnp
from jax import lax
from jax.experimental import pallas as pl
from jax.experimental.pallas import tpu as pltpu
from jax.sharding import PartitionSpec as P

EPS = 1e-06
STEPS = (19, 21, 24, 27, 31, 35, 40, 46, 52, 59, 67, 77, 87, 99, 113)


Z = 4


class Place:
    def __init__(self, rep, fsdp):
        self.rep, self.fsdp = rep, fsdp
        self.nx = fsdp // Z
        r = lax.axis_index("rep")
        f = lax.axis_index("fsdp")
        self.c, self.y = r % 2, (r // 2) % 2
        self.z, self.x = f // self.nx, f % self.nx
        self.q = 2 * self.y + self.c

    def core(self, v):
        return lax.ppermute(v, "rep", [(i, i ^ 1) for i in range(self.rep)])

    def across(self, v, bit):
        return lax.ppermute(v, "rep", [(i, i ^ bit) for i in range(self.rep)])

    def along_x(self, v, d):
        nx = self.nx
        return lax.ppermute(
            v, "fsdp", [(i, i // nx * nx + (i % nx + d) % nx) for i in range(self.fsdp)]
        )

    def along_z(self, v, d):
        return lax.ppermute(
            v, "fsdp", [(i, (i + d * self.nx) % self.fsdp) for i in range(self.fsdp)]
        )


def low(v):
    return v.astype(jnp.bfloat16)


def wide(v):
    return v.astype(jnp.float32)


def pick(v, i, axis=0):
    return lax.dynamic_index_in_dim(v, i, axis, keepdims=False)


FREE = pl.CostEstimate(flops=0, bytes_accessed=0, transcendentals=0)


def lasting(microseconds):
    return pl.CostEstimate(
        flops=int(microseconds * 1e9), bytes_accessed=0, transcendentals=0
    )


VMEM = pl.BlockSpec(memory_space=pltpu.VMEM)
SMEM = pl.BlockSpec(memory_space=pltpu.SMEM)


def shape_of(shape, dtype=jnp.bfloat16):
    return jax.ShapeDtypeStruct(shape, dtype)


def call(body, ins, outs, name, waits=(), specs=None, vmem=16, cost=FREE, **kw):
    waits = list(waits)
    count, late = len(ins), len(ins) + len(waits)

    def kernel(*refs):
        body(*refs[:count], *refs[late:])

    return pl.pallas_call(
        kernel,
        in_specs=list(specs or [VMEM] * count) + [pl.BlockSpec(memory_space=pl.ANY)] * len(waits),
        out_shape=outs,
        name=name,
        compiler_params=pltpu.CompilerParams(vmem_limit_bytes=vmem * 1024 * 1024),
        cost_estimate=cost,
        **kw,
    )(*ins, *waits)


def stack_kernel(*refs):
    for k, ref in enumerate(refs[:-1]):
        refs[-1][k] = ref[...]


def copy_kernel(ref, out):
    out[...] = ref[...]


def stacked(values, waits=()):
    shape = shape_of((len(values),) + values[0].shape, values[0].dtype)
    return call(stack_kernel, values, shape, "stack", waits)


def held_back(value, waits):
    return call(copy_kernel, [value], shape_of(value.shape, value.dtype), "hold", waits)


LANES = 128
SMALL_ROWS = 16


def assemble_kernel(where_ref, *refs, parts, nx, sizes, small):
    outs = refs[len(parts) :]
    c, y, z, x = (where_ref[i] for i in range(4))
    for ref, (dc, dy, dx) in zip(refs, parts):
        core = c ^ dc
        row = y ^ dy
        col = lax.rem(x - dx + nx, nx)
        for k in range(Z):
            f = lax.rem(z - k + Z, Z) * nx + col
            at = 0
            for out, (m, h, w) in zip(outs, sizes):
                for t in range(w // LANES):
                    lane = pl.ds(pl.multiple_of(core * w + t * LANES, LANES), LANES)
                    for i in range(m):
                        out[i, f, row, :, lane] = ref[k, at : at + h, :]
                        at += h
            if small and (dc, dy) == (0, 0):
                outs[-1][f] = ref[k, at : at + SMALL_ROWS, :]


class Gather:
    def __init__(self, place, shards, y_last, small=None):
        self.place, self.y_last, self.small = place, y_last, small
        self.sizes, rows = [], []
        for shard in shards:
            m, h, w = shard.shape[0], shard.shape[1] // 2, shard.shape[2] // 2
            self.sizes.append((m, h, w))
            cut = lax.dynamic_slice(shard, (0, place.y * h, place.c * w), (m, h, w))
            cut = jnp.transpose(cut.reshape(m, h, w // LANES, LANES), (2, 0, 1, 3))
            rows.append(cut.reshape(-1, LANES))
        if small is not None:
            rows.append(small)
        self.piece = rows[0] if len(rows) == 1 else jnp.concatenate(rows)

    def first(self):
        self.pieces = [self.piece] + [self.place.along_z(self.piece, d) for d in range(1, Z)]

    def second(self, *waits):
        self.stack = stacked(self.pieces, waits)

    def send(self):
        place, stack = self.place, self.stack
        self.held = {(0, 0): stack}
        for d in range(1, place.nx):
            self.held[0, d] = place.along_x(stack, d)
        self.held[1, 0] = place.across(stack, 2)

    def turn(self, *waits):
        self.onward = []
        for d in range(1, self.place.nx) if self.y_last else (0,):
            key = (0, d) if self.y_last else (1, 0)
            if waits:
                self.held[key] = held_back(self.held[key], waits)
            self.onward.append(self.held[key])

    def third(self):
        place, nx = self.place, self.place.nx
        for d in range(1, nx):
            if self.y_last:
                self.held[1, d] = place.across(self.held[0, d], 2)
            else:
                self.held[1, d] = place.along_x(self.held[1, 0], d)

    def settle(self, *waits):
        for d in range(1, self.place.nx):
            self.held[1, d] = held_back(self.held[1, d], waits)

    def whole(self, *waits):
        place = self.place
        parts, arrays = [], []
        for key, value in self.held.items():
            parts += [(0,) + key, (1,) + key]
            arrays += [value, place.across(value, 1)]
        shapes = [shape_of((m, place.fsdp, 2, h, 2 * w)) for m, h, w in self.sizes]
        if self.small is not None:
            shapes.append(shape_of((place.fsdp, SMALL_ROWS, LANES)))
        where = jnp.stack([place.c, place.y, place.z, place.x]).astype(jnp.int32)
        body = functools.partial(
            assemble_kernel,
            parts=tuple(parts),
            nx=place.nx,
            sizes=tuple(self.sizes),
            small=self.small is not None,
        )
        specs = [SMEM] + [VMEM] * len(arrays)
        full = call(body, [where] + arrays, shapes, "assemble", waits, specs, vmem=28)
        whole = [
            v.reshape(m, place.fsdp * 2 * h, 2 * w) for v, (m, h, w) in zip(full, self.sizes)
        ]
        return whole + list(full[len(whole) :])


def step_kernel(where_ref, kept_ref, *refs, axis, count, lead):
    got, keep_ref, send_refs = refs[: -count], refs[-count], refs[len(refs) - count + 1 :]
    own = where_ref[0]
    rest = [()]
    for size in lead[:axis] + lead[axis + 1 :]:
        rest = [r + (i,) for r in rest for i in range(size)]

    def value(at):
        total = kept_ref[at]
        for ref in got:
            total = total + ref[at].astype(jnp.float32)
        return total

    for r in rest:
        keep_ref[r] = value(r[:axis] + (own,) + r[axis:])
        for d, ref in enumerate(send_refs, 1):
            there = lax.rem(own + d, count)
            ref[r] = value(r[:axis] + (there,) + r[axis:]).astype(jnp.bfloat16)


def total_kernel(kept_ref, *refs):
    total = kept_ref[...]
    for ref in refs[:-1]:
        total = total + ref[...].astype(jnp.float32)
    refs[-1][...] = total


def rows_kernel(where_ref, total_ref, other_ref, out):
    h = total_ref.shape[0]
    y = where_ref[0]
    out[pl.ds(pl.multiple_of(y * h, 8), h), :] = total_ref[...]
    out[pl.ds(pl.multiple_of((1 - y) * h, 8), h), :] = other_ref[...]


class Reduce:
    def __init__(self, place, sent, kept):
        self.place = place
        lead = (Z, place.nx, 2)
        self.sent = [sent]
        self.kept = kept.reshape(lead + kept.shape[2:])
        self.axes = ["z", "x", "y"]
        self.name = "core"

    def send(self):
        place = self.place
        if self.name == "core":
            self.got = [place.across(self.sent[0], 1).reshape(self.kept.shape)]
        elif self.name == "y":
            self.got = [place.across(self.sent[0], 2)]
        else:
            move = place.along_x if self.name == "x" else place.along_z
            self.got = [move(v, d) for d, v in enumerate(self.sent, 1)]

    def step(self, name, *waits, cost=FREE):
        place = self.place
        axis = self.axes.index(name)
        lead, tail = self.kept.shape[:-2], self.kept.shape[-2:]
        count = lead[axis]
        left = lead[:axis] + lead[axis + 1 :] + tail
        own = {"z": place.z, "x": place.x, "y": place.y}[name].reshape(1).astype(jnp.int32)
        outs = [shape_of(left, jnp.float32)] + [shape_of(left)] * (count - 1)
        body = functools.partial(step_kernel, axis=axis, count=count, lead=lead)
        ins = [own, self.kept] + self.got
        specs = [SMEM] + [VMEM] * (len(ins) - 1)
        self.kept, *self.sent = call(
            body, ins, outs, "step_" + name, waits, specs, vmem=20, cost=cost
        )
        self.axes.remove(name)
        self.name = name

    def finish(self, *waits, cost=FREE):
        place = self.place
        shape = shape_of(self.kept.shape, jnp.float32)
        total = call(total_kernel, [self.kept] + self.got, shape, "total", waits, cost=cost)
        bit = 4
        while bit < place.rep:
            total = total + place.across(total, bit)
            bit *= 2
        self.total, self.other = total, place.across(total, 2)

    def rows(self, *waits, cost=FREE):
        place = self.place
        h, w = self.total.shape
        ins = [place.y.reshape(1).astype(jnp.int32), self.total, self.other]
        out = shape_of((2 * h, w), jnp.float32)
        self.near = call(rows_kernel, ins, out, "rows", waits, [SMEM, VMEM, VMEM], cost=cost)
        self.far = place.across(self.near, 1)

    def done(self):
        first = self.place.c == 0
        return jnp.where(first, self.near, self.far), jnp.where(first, self.far, self.near)


def sum_replicas(place, partial):
    bit = 1
    while bit < place.rep:
        partial = partial + place.across(partial, bit)
        bit *= 2
    return partial


def sum_owners(place, partial):
    total = partial.reshape(Z, place.nx, -1)
    near = pick(total, place.x, 1)
    for d in range(1, place.nx):
        near = near + place.along_x(pick(total, (place.x + d) % place.nx, 1), d)
    mine = pick(near, place.z)
    for d in range(1, Z):
        mine = mine + place.along_z(pick(near, (place.z + d) % Z), d)
    return mine


NEGATIVE = -1e30
TILE = 256
PAIR = 128


def dot(a, b, dims):
    return lax.dot_general(a, b, (dims, ((), ())), preferred_element_type=jnp.float32)


NT = ((1,), (1,))
NN = ((1,), (0,))
TN = ((0,), (0,))


def turned(v):
    return v.astype(jnp.float32).T


def half_mask(j):
    return lax.broadcasted_iota(jnp.int32, (1, PAIR), 1) // (PAIR // 2) == j


def masked_scores(k, qm, toe, length, t, causal):
    scores = dot(k, qm, NT)
    rows = scores.shape[0]
    key = lax.broadcasted_iota(jnp.int32, (rows, TILE), 0)
    if causal:
        bias = toe[:, :TILE]
        if t:
            bias = jnp.concatenate([toe[:, TILE:], bias], axis=0)
        scores = scores + bias
        query = lax.broadcasted_iota(jnp.int32, (rows, TILE), 1) + t * TILE
        allowed = key <= jnp.minimum(query, length - 1)
    else:
        allowed = key < length
    return jnp.where(allowed, scores, NEGATIVE)


def spread(row_ref, toe_ref):
    for j in range(2):
        row = jnp.broadcast_to(row_ref[0, j : j + 1, :], (TILE, 2 * TILE))
        toe_ref[j] = pltpu.roll(row, 0, 1, stride=1, stride_axis=0)


def forward_kernel(causal, len_ref, *refs):
    if causal:
        q_ref, k_ref, v_ref, row_ref, o_ref, lse_ref, toe_ref = refs
    else:
        q_ref, k_ref, v_ref, o_ref, lse_ref = refs
        toe_ref = None
    s = pl.program_id(1)
    length = len_ref[s]
    if causal:

        @pl.when(s == 0)
        def _():
            spread(row_ref, toe_ref)

    q, k, v = q_ref[0], k_ref[0], v_ref[0]
    v_turned = turned(v).astype(jnp.bfloat16)
    cells = [(t, j) for t in range(q.shape[0] // TILE) for j in range(2)]

    def score(t, j):
        seen = (t + 1) * TILE if causal else k.shape[0]
        qm = jnp.where(half_mask(j), q[t * TILE : (t + 1) * TILE], 0)
        return masked_scores(k[:seen], qm, toe_ref[j] if causal else None, length, t, causal)

    outs = []
    ahead = score(*cells[0])
    for i, (t, j) in enumerate(cells):
        scores = ahead
        if i + 1 < len(cells):
            ahead = score(*cells[i + 1])
        here = slice(t * TILE, (t + 1) * TILE)
        top = jnp.max(scores, axis=0, keepdims=True)
        grown = jnp.exp(scores - top)
        total = jnp.sum(grown, axis=0, keepdims=True)
        lse_ref[0, 0, j : j + 1, here] = top + jnp.log(total)
        chances = (grown * (1.0 / total)).astype(jnp.bfloat16)
        outs.append(dot(v_turned[j * 64 : (j + 1) * 64, : scores.shape[0]], chances, NN))
        if j:
            o_ref[0, here, :] = turned(jnp.concatenate(outs, axis=0)).astype(jnp.bfloat16)
            outs = []


def diagonal_sums(v):
    width = v.shape[1]
    groups = v[:8]
    for a in range(8, v.shape[0], 8):
        groups = groups + pltpu.roll(v[a : a + 8], width - a, 1)
    total = groups[:1]
    for b in range(1, 8):
        total = total + pltpu.roll(groups[b : b + 1], width - b, 1)
    return total


def backward_kernel(causal, len_ref, *refs):
    if causal:
        q_ref, k_ref, v_ref, do_ref, lse_ref, row_ref = refs[:6]
        dq_ref, dk_ref, dv_ref, diag_ref, toe_ref, sum_ref = refs[6:]
    else:
        q_ref, k_ref, v_ref, do_ref, lse_ref = refs[:5]
        dq_ref, dk_ref, dv_ref = refs[5:]
        toe_ref = None
    s = pl.program_id(1)
    length = len_ref[s]
    if causal:

        @pl.when(s == 0)
        def _():
            spread(row_ref, toe_ref)
            sum_ref[...] = jnp.zeros_like(sum_ref)

    q, k, v, do = q_ref[0], k_ref[0], v_ref[0], do_ref[0]
    k_turned = turned(k).astype(jnp.bfloat16)
    tiles = q.shape[0] // TILE
    dk = [None] * tiles
    dv = [None] * tiles
    cells = [(t, j) for t in range(tiles) for j in range(2)]
    outs = []

    def add(held, value):
        return value if held is None else held + value

    def score(t, j):
        seen = (t + 1) * TILE if causal else k.shape[0]
        here = slice(t * TILE, (t + 1) * TILE)
        qm = jnp.where(half_mask(j), q[here], 0)
        dom = jnp.where(half_mask(j), do[here], 0)
        scores = masked_scores(k[:seen], qm, toe_ref[j] if causal else None, length, t, causal)
        return scores, dot(v[:seen], dom, NT), qm, dom

    def finish(t, j, chances, d_scores, qm, dom):
        seen = d_scores.shape[0]
        outs.append(dot(k_turned[j * 64 : (j + 1) * 64, :seen], d_scores, NN))
        dv_part = dot(chances, dom, NN)
        dk_part = dot(d_scores, qm, NN)
        for b in range(seen // TILE):
            rows = slice(b * TILE, (b + 1) * TILE)
            dv[b] = add(dv[b], dv_part[rows])
            dk[b] = add(dk[b], dk_part[rows])
        if causal:
            if t:
                sum_ref[j, :, TILE:] += d_scores[: t * TILE].astype(jnp.float32)
            sum_ref[j, :, :TILE] += d_scores[t * TILE :].astype(jnp.float32)
        if j:
            here = slice(t * TILE, (t + 1) * TILE)
            dq_ref[0, here, :] = turned(jnp.concatenate(outs, axis=0)).astype(jnp.bfloat16)
            outs.clear()

    ahead = score(*cells[0])
    behind = None
    for i, (t, j) in enumerate(cells):
        scores, d_chances, qm, dom = ahead
        if i + 1 < len(cells):
            ahead = score(*cells[i + 1])
        here = slice(t * TILE, (t + 1) * TILE)
        chances = jnp.exp(scores - lse_ref[0, 0, j : j + 1, here])
        delta = jnp.sum(chances * d_chances, axis=0, keepdims=True)
        d_scores = (chances * (d_chances - delta)).astype(jnp.bfloat16)
        if behind is not None:
            finish(*behind)
        behind = (t, j, chances.astype(jnp.bfloat16), d_scores, qm, dom)
    finish(*behind)
    for b in range(tiles):
        rows = slice(b * TILE, (b + 1) * TILE)
        dk_ref[0, rows, :] = dk[b].astype(jnp.bfloat16)
        dv_ref[0, rows, :] = dv[b].astype(jnp.bfloat16)
    if causal:

        @pl.when(s == pl.num_programs(1) - 1)
        def _():
            for j in range(2):
                diag_ref[0, j : j + 1, :] = diagonal_sums(sum_ref[j])


def attend(kind, q, k, v, lengths, row=None, do=None, lse=None, waits=()):
    count, slots, width = q.shape
    pairs = width // PAIR
    assert slots == 2 * TILE and k.shape[1] == 2 * TILE
    block = pl.BlockSpec((1, slots, PAIR), lambda p, s: (s, 0, p))
    lse_block = pl.BlockSpec((1, 1, 2, slots), lambda p, s: (s, p, 0, 0))
    row_block = pl.BlockSpec((1, 2, slots), lambda p, s: (p, 0, 0))
    state = jax.ShapeDtypeStruct(q.shape, jnp.bfloat16)
    causal = row is not None
    ins, specs = [lengths, q, k, v], [pl.BlockSpec(memory_space=pltpu.SMEM), block, block, block]
    if kind == "forward":
        body = forward_kernel
        outs = [state, jax.ShapeDtypeStruct((count, pairs, 2, slots), jnp.float32)]
        out_specs = [block, lse_block]
    else:
        body = backward_kernel
        ins += [do, lse]
        specs += [block, lse_block]
        outs = [state] * 3
        out_specs = [block] * 3
    scratch = []
    if causal:
        ins.append(row)
        specs.append(row_block)
        scratch.append(pltpu.VMEM((2, TILE, 2 * TILE), jnp.float32))
        if kind == "backward":
            outs.append(jax.ShapeDtypeStruct(row.shape, jnp.float32))
            out_specs.append(row_block)
            scratch.append(pltpu.VMEM((2, TILE, 2 * TILE), jnp.float32))
    return call(
        functools.partial(body, causal),
        ins,
        outs,
        ("self_" if causal else "cross_") + kind,
        waits,
        specs,
        vmem=16,
        cost=lasting(200),
        grid=(pairs, count),
        out_specs=out_specs,
        scratch_shapes=scratch,
    )


FF_TILE = 256
ROW_TILE = 256


def feed_kernel(n_ref, df_ref, in_ref, out_ref, product_ref, gate_ref, up_ref):
    scale, cubic = 0.7978845608028654, 0.044715

    def dots(r):
        rows = slice(r * ROW_TILE, (r + 1) * ROW_TILE)
        n = n_ref[rows, :]
        return (
            dot(n, in_ref[0], NN),
            dot(n, in_ref[1], NN),
            dot(df_ref[rows, :], out_ref[...], NT),
        )

    count = n_ref.shape[0] // ROW_TILE
    ahead = dots(0)
    for r in range(count):
        gate, up, d_product = ahead
        if r + 1 < count:
            ahead = dots(r + 1)
        rows = slice(r * ROW_TILE, (r + 1) * ROW_TILE)
        square = gate * gate
        bend = jnp.tanh(scale * (gate + cubic * (square * gate)))
        half = 0.5 * (1.0 + bend)
        gelu = gate * half
        slope = half + (0.5 * scale) * gate * (1.0 - bend * bend) * (1.0 + 3 * cubic * square)
        product_ref[rows, :] = (gelu * up).astype(jnp.bfloat16)
        gate_ref[rows, :] = (d_product * up * slope).astype(jnp.bfloat16)
        up_ref[rows, :] = (d_product * gelu).astype(jnp.bfloat16)


def feed(n, df, ffin, ffout):
    count, width = n.shape
    hidden = ffout.shape[0]
    whole = pl.BlockSpec((count, width), lambda i: (0, 0))
    tile = pl.BlockSpec((count, FF_TILE), lambda i: (0, i))
    state = jax.ShapeDtypeStruct((count, hidden), jnp.bfloat16)
    specs = [
        whole,
        whole,
        pl.BlockSpec((2, width, FF_TILE), lambda i: (0, 0, i)),
        pl.BlockSpec((FF_TILE, width), lambda i: (i, 0)),
    ]
    return call(
        feed_kernel,
        [n, df, ffin, ffout],
        [state] * 3,
        "feed",
        (),
        specs,
        cost=lasting(100),
        vmem=24,
        grid=(hidden // FF_TILE,),
        out_specs=[tile] * 3,
    )


def matmuls_kernel(*refs, count, dims, ends):
    total = dot(refs[0][...], refs[count][0], dims)
    for i in range(1, count):
        total = total + dot(refs[i][...], refs[count + i][0], dims)
    if ends:
        total = (total + refs[2 * count][...]) * refs[2 * count + 1][...]
    refs[-1][...] = total.astype(refs[-1].dtype)


def matmuls(lefts, weights, dims, name, waits=(), ends=(), cost=FREE, dtype=jnp.float32):
    lefts = [v.reshape(-1, v.shape[-1]) for v in lefts]
    ends = [v.reshape(-1, v.shape[-1]) for v in ends]
    rows = lefts[0].shape[0]
    width = weights[0][0].shape[1 if dims == NT else 2]

    def tile(v):
        return pl.BlockSpec((ROW_TILE, v.shape[1]), lambda i: (i, 0))

    def layer(v, k):
        return pl.BlockSpec((1,) + v.shape[1:], lambda i: (k, 0, 0))

    out = shape_of((rows, width), dtype)
    return call(
        functools.partial(matmuls_kernel, count=len(lefts), dims=dims, ends=bool(ends)),
        lefts + [w for w, _ in weights] + ends,
        out,
        name,
        waits,
        [tile(v) for v in lefts] + [layer(*w) for w in weights] + [tile(v) for v in ends],
        vmem=24,
        cost=cost,
        grid=(rows // ROW_TILE,),
        out_specs=tile(out),
    )


def grads_kernel(where_ref, *refs, pairs, lefts, rights):
    left_refs, right_refs = refs[:lefts], refs[lefts : lefts + rights]
    sent_ref, kept_ref = refs[-2:]
    first = where_ref[0] == 0
    for i, left in enumerate(left_refs):
        for m in range(0, left.shape[1], ROW_TILE):
            rows = slice(m, m + ROW_TILE)
            block = turned(left[:, rows]).astype(jnp.bfloat16)
            at = 0
            for k, j in pairs:
                right = right_refs[j]
                w = right.shape[1] // 2
                if k == i:
                    both = dot(block, right[...], NN)
                    near, far = both[:, :w], both[:, w:]
                    sent_ref[rows, at : at + w] = jnp.where(first, far, near).astype(jnp.bfloat16)
                    kept_ref[rows, at : at + w] = jnp.where(first, near, far)
                at += w


def stage_grads(place, lefts, rights, pairs, *waits, cost=FREE):
    lefts = [v.reshape(-1, v.shape[-1]) for v in lefts]
    rights = [v.reshape(-1, v.shape[-1]) for v in rights]
    height = lefts[0].shape[1]
    width = sum(rights[j].shape[1] // 2 for _, j in pairs)
    ins = [place.c.reshape(1).astype(jnp.int32)] + lefts + rights
    sent, kept = call(
        functools.partial(
            grads_kernel, pairs=tuple(pairs), lefts=len(lefts), rights=len(rights)
        ),
        ins,
        [shape_of((height, width)), shape_of((height, width), jnp.float32)],
        "grads",
        waits,
        [SMEM] + [VMEM] * (len(ins) - 1),
        vmem=28,
        cost=cost,
    )
    shape = (place.fsdp, 2, height // place.fsdp // 2, width)
    return Reduce(place, sent.reshape(shape), kept.reshape(shape))


def rms_scale(values, factor):
    return values * lax.rsqrt(jnp.mean(values * values, axis=-1, keepdims=True) + EPS) * factor


def rms_back(values, factor, grad_out):
    return jax.vjp(rms_scale, values, factor)[1](grad_out)


def project(a, w):
    return jnp.einsum("vgq,qy->vgy", a, w, preferred_element_type=jnp.float32)


def project_back(a, w):
    return jnp.einsum("gjr,fr->gjf", a, w, preferred_element_type=jnp.float32)


def bucket_hot(extent, buckets):
    distance = jnp.arange(extent, dtype=jnp.int32)
    far = 16 + sum(((distance >= border).astype(jnp.int32) for border in STEPS))
    bucket = jnp.where(distance < 16, distance, far)
    return (bucket[:, None] == jnp.arange(buckets, dtype=jnp.int32)).astype(jnp.float32)


def per_device(
    rep,
    fsdp,
    tokens,
    encoder_states,
    cotangent,
    qkv_weight,
    out_weight,
    ffin_weight,
    ffout_weight,
    norm_gains,
    bias_table,
    lengths,
    enc_lengths,
):
    place = Place(rep, fsdp)
    seq_len, width = tokens.shape[1:]
    table_rows, heads = bias_table.shape
    shard = qkv_weight.shape[3]
    first = place.c == 0
    half = ffin_weight.shape[3] // 2
    part = width // 2

    small_count = 3 * shard + table_rows * heads
    small = jnp.concatenate([norm_gains.reshape(-1), bias_table.reshape(-1)])
    small = jnp.pad(small, (0, SMALL_ROWS * LANES - small_count)).reshape(SMALL_ROWS, LANES)
    stages = [
        Gather(place, [jnp.concatenate([qkv_weight[0, 0], out_weight[0, :1]])], True, small),
        Gather(place, [jnp.concatenate([qkv_weight[0, 1], out_weight[0, 1:]])], False),
        Gather(place, [ffin_weight[0], ffout_weight], True),
    ]
    for stage in stages:
        stage.first()
    stages[0].second()
    stages[0].send()
    stages[1].second()
    stages[0].turn(stages[1].stack, stages[0].held[1, 0])
    stages[0].third()
    stages[2].second()
    self_w, small = stages[0].whole(stages[2].stack)
    small = small.reshape(fsdp, SMALL_ROWS * LANES)
    gains = small[:, : 3 * shard].reshape(fsdp, 3, shard)
    gains = wide(jnp.transpose(gains, (1, 0, 2)).reshape(3, width))
    table = wide(small[:, 3 * shard : small_count].reshape(fsdp * table_rows, heads))
    hot = bucket_hot(seq_len, fsdp * table_rows)
    row = jnp.einsum("nb,bh->hn", hot, table, precision=lax.Precision.HIGHEST)
    row = row.reshape(heads // 2, 2, seq_len)

    live = wide(jnp.arange(seq_len, dtype=jnp.int32)[None, :] < lengths[:, None])[:, :, None]
    stream = wide(tokens)
    normed_self = low(rms_scale(stream, gains[0]))
    q1, k1, v1 = (low(project(normed_self, self_w[i])) for i in range(3))
    stages[1].send()
    stages[1].turn(self_w)
    stages[1].third()
    stages[2].send()
    ready = stages[1].onward + [stages[2].stack]
    o1, lse1 = attend("forward", q1, k1, v1, lengths, row, waits=ready)
    middle = stream + project(o1, self_w[3])
    normed_cross = low(rms_scale(middle, gains[1]))
    cross_w, = stages[1].whole(o1)
    q2 = low(project(normed_cross, cross_w[0]))
    k2, v2 = (low(project(encoder_states, cross_w[i])) for i in (1, 2))
    stages[2].turn(cross_w)
    stages[2].third()
    o2, lse2 = attend("forward", q2, k2, v2, enc_lengths, waits=stages[2].onward)
    later = middle + project(o2, cross_w[3])
    normed_feed = low(rms_scale(later, gains[2]))
    stages[2].settle(o2)
    ffin, ffout = stages[2].whole(o2)

    def flat(v):
        return v.reshape(-1, v.shape[-1])

    grad = wide(cotangent) * live
    grad_low = low(grad)
    product, grad_gate, grad_upward = (
        v.reshape(tokens.shape[:2] + (2 * half,))
        for v in feed(flat(normed_feed), flat(grad_low), ffin, ffout[0])
    )

    ffin_sum = stage_grads(place, [normed_feed], [grad_gate, grad_upward], [(0, 0), (0, 1)])
    ffin_sum.send()
    ffout_sum = stage_grads(place, [product], [grad_low], [(0, 0)], *ffin_sum.sent)
    ffin_sum.step("x", *ffout_sum.sent)
    ffout_sum.send()
    grad_normed = matmuls(
        [grad_gate, grad_upward], [(ffin, 0), (ffin, 1)], NT, "grad_normed", ffin_sum.sent, cost=lasting(100)
    ).reshape(tokens.shape)
    grad_norm, gain_feed = rms_back(later, gains[2], grad_normed)
    grad_later = grad + grad_norm
    ffout_sum.step("y", *ffin_sum.sent)

    da2 = low(grad_later)
    do = low(project_back(da2, cross_w[3]))
    ready = ffout_sum.sent + ffin_sum.sent
    ffin_sum.send()
    ffout_sum.send()
    dq2, dk2, dv2 = attend("backward", q2, k2, v2, enc_lengths, None, do, lse2, ready)
    ffin_sum.step("y", dq2)
    ffout_sum.step("x", *ffin_sum.sent)
    ffin_sum.send()
    ffout_sum.send()
    grad_norm, gain_cross = rms_back(middle, gains[1], project_back(dq2, cross_w[0]))
    grad_middle = grad_later + grad_norm
    da1 = low(grad_middle)
    cross_sum = stage_grads(
        place,
        [normed_cross, encoder_states, o2, o1],
        [dq2, dk2, dv2, da2, da1],
        [(0, 0), (1, 1), (1, 2), (2, 3), (3, 4)],
        *ffout_sum.sent,
        cost=lasting(100),
    )
    cross_sum.send()
    ffin_sum.step("z", *cross_sum.sent)
    do = matmuls(
        [da1],
        [(self_w, 3)],
        NT,
        "self_do",
        ffin_sum.sent,
        cost=lasting(100),
        dtype=jnp.bfloat16,
    ).reshape(tokens.shape)
    cross_sum.step("y", do)

    ready = cross_sum.sent + ffin_sum.sent
    cross_sum.send()
    ffin_sum.send()
    dq1, dk1, dv1, diagonals = attend("backward", q1, k1, v1, lengths, row, do, lse1, ready)
    self_sum = stage_grads(
        place, [normed_self], [dq1, dk1, dv1], [(0, 0), (0, 1), (0, 2)]
    )
    self_sum.send()
    cross_sum.step("x", *self_sum.sent)
    cross_sum.send()
    ffout_sum.step("z", *cross_sum.sent, cost=lasting(100))
    ffin_sum.finish(*ffout_sum.sent)
    ffout_sum.send()
    self_sum.step("y", *ffout_sum.sent)
    self_sum.send()
    encoder_grad = matmuls(
        [dk2, dv2],
        [(cross_w, 1), (cross_w, 2)],
        NT,
        "encoder_grad",
        self_sum.sent,
        cost=lasting(100),
    ).reshape(tokens.shape)
    into = matmuls(
        [dq1, dk1, dv1],
        [(self_w, 0), (self_w, 1), (self_w, 2)],
        NT,
        "into",
        [encoder_grad, ffin_sum.total],
    ).reshape(tokens.shape)
    cross_sum.step("z", into)
    cross_sum.send()
    self_sum.step("x", *cross_sum.sent)
    self_sum.send()
    grad_norm, gain_self = rms_back(stream, gains[0], into)
    token_grad = grad_middle + grad_norm
    ffout_sum.finish(*self_sum.sent, cost=lasting(100))
    ffin_sum.rows(ffout_sum.total)
    output_state = matmuls(
        [product],
        [(ffout, 0)],
        NN,
        "output_state",
        [ffout_sum.total, ffin_sum.near],
        [later, jnp.broadcast_to(live, tokens.shape[:2] + (1,))],
    ).reshape(tokens.shape)
    self_sum.step("z", output_state)
    self_sum.send()
    cross_sum.finish(*self_sum.sent, cost=lasting(100))
    diagonals = held_back(diagonals, [output_state])
    grad_table = jnp.einsum(
        "nb,hn->bh", hot, diagonals.reshape(heads, seq_len), precision=lax.Precision.HIGHEST
    )
    small = jnp.stack([gain_self, gain_cross, gain_feed]).reshape(3, fsdp, shard)
    small = jnp.concatenate(
        [
            jnp.transpose(small, (1, 0, 2)).reshape(fsdp, 3 * shard),
            grad_table.reshape(fsdp, table_rows * heads),
        ],
        axis=1,
    )
    small = held_back(jnp.pad(small, ((0, 0), (0, -small_count % 128))), self_sum.sent)
    small = sum_owners(place, sum_replicas(place, small))
    ffout_sum.rows(cross_sum.total)
    cross_sum.rows(ffout_sum.near)
    self_sum.finish(cross_sum.near)
    self_sum.rows()

    def matrices(stage, size):
        near, far = stage.done()
        return [
            jnp.concatenate([near[:, i : i + size], far[:, i : i + size]], axis=1)
            for i in range(0, near.shape[1], size)
        ]

    cross_grads = matrices(cross_sum, part)
    self_grads = matrices(self_sum, part)
    qkv_grad = jnp.stack([jnp.stack(self_grads), jnp.stack(cross_grads[:3])])[None]
    out_grad = jnp.stack([cross_grads[4], cross_grads[3]])[None]
    ffin_grad = jnp.stack(matrices(ffin_sum, half))[None]
    ffout_grad = matrices(ffout_sum, part)[0][None]
    return (
        output_state,
        token_grad,
        encoder_grad,
        qkv_grad,
        out_grad,
        ffin_grad,
        ffout_grad,
        small[: 3 * shard].reshape(1, 3, shard),
        small[3 * shard : small_count].reshape(table_rows, heads),
    )


def solution(mesh):
    in_specs = (
        P(("rep", "fsdp"), None, None),
        P(("rep", "fsdp"), None, None),
        P(("rep", "fsdp"), None, None),
        P(None, None, None, "fsdp", None),
        P(None, None, "fsdp", None),
        P(None, None, "fsdp", None),
        P(None, "fsdp", None),
        P(None, None, "fsdp"),
        P("fsdp", None),
        P(("rep", "fsdp")),
        P(("rep", "fsdp")),
    )
    out_specs = (
        P(("rep", "fsdp"), None, None),
        P(("rep", "fsdp"), None, None),
        P(("rep", "fsdp"), None, None),
        P(None, None, None, "fsdp", None),
        P(None, None, "fsdp", None),
        P(None, None, "fsdp", None),
        P(None, "fsdp", None),
        P(None, None, "fsdp"),
        P("fsdp", None),
    )
    return jax.shard_map(
        functools.partial(per_device, mesh.shape["rep"], mesh.shape["fsdp"]),
        mesh=mesh, in_specs=in_specs, out_specs=out_specs, check_vma=False
    )
```
